512 devices in a mesh: rows: 128 (over y, z, core), rep: 4 (over x).
Axes of the slice: x: 4, y: 8, z: 8, core: 2. Of those that a mesh axis runs over, the one named last changes fastest.
Arguments:
- tables: bfloat16 [262144, 128], P('rows'), may hold values from -0.5 to 0.5
- indices: int32 [8192, 8, 8], P(('rows', 'rep')), may hold values from 0 to 32767
- bag_lengths: int32 [8192, 8], P(('rows', 'rep')), may hold values from 1 to 8
- dense: bfloat16 [8192, 13], P(('rows', 'rep')), may hold values from -6 to 6
- bottom_first: bfloat16 [13, 512], replicated, may hold values from -1.75 to 1.75
- bottom_second: bfloat16 [512, 256], replicated, may hold values from -0.375 to 0.375
- bottom_third: bfloat16 [256, 128], replicated, may hold values from -0.5 to 0.5
- top_first: bfloat16 [164, 1024], P(None, 'rep'), may hold values from -0.5 to 0.5
- top_second: bfloat16 [1024, 1024], P(None, 'rep'), may hold values from -0.25 to 0.25
- top_third: bfloat16 [1024, 512], P(None, 'rep'), may hold values from -0.25 to 0.25
- top_fourth: bfloat16 [512, 256], P(None, 'rep'), may hold values from -0.375 to 0.375
- top_last: bfloat16 [256], replicated, may hold values from -0.5 to 0.5
Outputs:
- logit: float32 [8192], P(('rows', 'rep'))
The draws below stay inside these ranges and needn't reach their ends.
Inputs may be any that keep to these rules, and one draw needn't show every extreme that they name: `indices`: each entry is a row number within its own table; entries at positions of a bag at or past its length are ignored.
All inputs are finite; a program needn't handle non-finite values.
Results may differ from the reference program's by a relative error of at most 0.0076.
Values may be sent and summed in bfloat16 or wider, within the bound.
No kernel may reach another device: no remote copies, remote signals or barrier semaphores. Data moves between devices by JAX's collectives and lax.ppermute only.
A program may use at most 64 MiB of HBM per device.

```python
import math
import jax
import jax.numpy as jnp
import numpy as np
from jax import lax

E = 128
DENSE = 13
H1 = 512
H2 = 256
T1 = 1024
T2 = 1024
T3 = 512
T4 = 256
TAB = 8
HOT = 8
TROWS = 32768
NPAIR = 36
BATCH = 8192


def place_ends(values, own_key, least, largest):
    longest = values.shape.index(max(values.shape))
    spots = []
    for shift in (0, 1):
        where = [jax.random.randint(jax.random.fold_in(own_key, axis), (), 0, length) for axis, length in enumerate(values.shape)]
        where[longest] = (where[longest] + shift) % values.shape[longest]
        spots.append(tuple(where))
    return values.at[spots[0]].set(least).at[spots[1]].set(largest)


def levels(own_key, dims, split, smallest, top_value):
    def one(position, blocks):
        heights = jax.random.uniform(jax.random.fold_in(jax.random.fold_in(own_key, 6), position), (blocks,), jnp.float32, smallest / len(split), top_value / len(split))
        return jnp.repeat(jnp.exp(heights), dims[position] // blocks).reshape((-1,) + (1,) * (len(dims) - position - 1))

    level = one(*split[0])
    for cut in split[1:]:
        level = level * one(*cut)
    return level


def rank_table(amount, lean):
    weights = [(1 << 20) // math.isqrt(grade ** lean) + 1 for grade in range(1, amount + 1)]
    spread = 1 + sum(weights) // (1 << 30)
    return np.cumsum(np.array([max(1, weight // spread) for weight in weights]))


def skewed_ids(key, extent, number_of, lean):
    table = rank_table(number_of, lean)
    ticket = jax.random.randint(jax.random.fold_in(key, 1), extent, 0, int(table[number_of - 1]))
    grade = jnp.searchsorted(jnp.asarray(table, jnp.int32), ticket, side="right")
    return jax.random.permutation(jax.random.fold_in(key, 2), number_of)[grade].astype(jnp.int32)


def centred(key, dims, deviation, limit, cuts=(), kind=jnp.bfloat16):
    gain = levels(key, dims, cuts, -0.22, 0.18) if cuts else 1.0
    drawn = jax.random.normal(key, dims, jnp.float32) * deviation * gain
    return jnp.minimum(jnp.maximum(drawn, -limit), limit).astype(kind)


def setup_inputs(seed: int = 0) -> dict:
    keys = jax.random.split(jax.random.key(seed), 13)
    return {
        "tables": centred(keys[0], (TAB * TROWS, E), E ** -0.5, 0.5, ((0, 128),)),
        "indices": place_ends(skewed_ids(keys[1], (BATCH, TAB, HOT), TROWS, 2), jax.random.fold_in(keys[1], 3), 0, TROWS - 1).astype(jnp.int32),
        "bag_lengths": place_ends(jax.random.randint(keys[2], (BATCH, TAB), 1, HOT + 1), jax.random.fold_in(keys[2], 1), 1, HOT).astype(jnp.int32),
        "dense": centred(keys[3], (BATCH, DENSE), 1.0, 6.0, ((0, 512),)),
        "bottom_first": centred(keys[4], (DENSE, H1), DENSE ** -0.5, 1.75),
        "bottom_second": centred(keys[5], (H1, H2), (H1 // 2) ** -0.5, 0.375),
        "bottom_third": centred(keys[6], (H2, E), (H2 // 2) ** -0.5, 0.5),
        "top_first": centred(keys[7], (E + NPAIR, T1), (E + NPAIR) ** -0.5, 0.5, ((1, 4),)),
        "top_second": centred(keys[8], (T1, T2), (T1 // 2) ** -0.5, 0.25, ((1, 4),)),
        "top_third": centred(keys[9], (T2, T3), (T2 // 2) ** -0.5, 0.25, ((1, 4),)),
        "top_fourth": centred(keys[10], (T3, T4), (T3 // 2) ** -0.5, 0.375, ((1, 4),)),
        "top_last": centred(keys[11], (T4,), (T4 // 2) ** -0.5, 0.5),
    }


def interact(bottom_out, pooled):
    features = jnp.concatenate([bottom_out[None], pooled], axis=0)
    gram_matrix = jnp.einsum("ibe,jbe->bij", features, features, precision=lax.Precision.HIGHEST)
    left_ids, right_ids = np.triu_indices(TAB + 1, 1)
    pair_dots = gram_matrix[:, left_ids, right_ids]
    return jnp.concatenate([bottom_out, pair_dots], axis=1).astype(jnp.bfloat16)


def bottom_net(dense, bottom_first, bottom_second, bottom_third):
    lower_act = jax.nn.relu(jnp.dot(dense, bottom_first, preferred_element_type=jnp.float32)).astype(jnp.bfloat16)
    middle = jax.nn.relu(jnp.dot(lower_act, bottom_second, preferred_element_type=jnp.float32)).astype(jnp.bfloat16)
    return jax.nn.relu(jnp.dot(middle, bottom_third, preferred_element_type=jnp.float32))


def reference(tables, indices, bag_lengths, dense, bottom_first, bottom_second, bottom_third, top_first, top_second, top_third, top_fourth, top_last):
    def pool_one(carried):
        table_num, table_idx, table_len = carried
        row_ids = (table_num * TROWS + table_idx).astype(jnp.int32)
        live_mask = jnp.arange(HOT, dtype=jnp.int32)[None, :] < table_len[:, None]
        picked = jnp.take(tables, row_ids, axis=0).astype(jnp.float32)
        return jnp.sum(jnp.where(live_mask[:, :, None], picked, jnp.zeros_like(picked)), axis=1)

    pooled = lax.map(pool_one, (jnp.arange(TAB, dtype=jnp.int32), jnp.transpose(indices, (1, 0, 2)), jnp.transpose(bag_lengths)))
    bottom_out = bottom_net(dense, bottom_first, bottom_second, bottom_third)
    activation = interact(bottom_out, pooled)
    for weight_mat in (top_first, top_second, top_third, top_fourth):
        activation = jax.nn.relu(jnp.dot(activation, weight_mat, preferred_element_type=jnp.float32)).astype(jnp.bfloat16)
    return jnp.dot(activation, top_last, preferred_element_type=jnp.float32)
```

```python
import functools

import jax
import jax.numpy as jnp
from jax import lax
from jax.experimental import pallas as pl
from jax.experimental.pallas import tpu as pltpu
from jax.sharding import Mesh
from jax.sharding import PartitionSpec as P

TAB = 8
HOT = 8
Y, Z, C, X = "y", "z", "c", "x"
ALL = (Y, Z, C, X)
LO = 256
GROUP = 2
HEAD_ROWS = 128
BF = jnp.bfloat16
F32 = jnp.float32
VM = pl.BlockSpec(memory_space=pltpu.VMEM)
SM = pl.BlockSpec(memory_space=pltpu.SMEM)
LANES = (((1,), (1,)), ((), ()))


def mm(a, b):
    return jnp.dot(a, b, preferred_element_type=F32)


def mm_t(a, b):
    return lax.dot_general(a, b, LANES, preferred_element_type=F32)


def relu(a):
    return jnp.maximum(a, 0.0)


def cost(micros):
    return pl.CostEstimate(flops=int(micros * 1.0e9), bytes_accessed=1 << 20, transcendentals=0)


def params(mib):
    return pltpu.CompilerParams(vmem_limit_bytes=mib << 20)


def prepare_kernel(peers, idx_ref, len_ref, out_ref):
    lens = len_ref[...]
    parts = [jnp.where(lens > h, idx_ref[:, h, :], -1) for h in range(HOT)]
    rows = jnp.concatenate(parts, axis=1)
    for t in range(TAB):
        out_ref[t * peers : (t + 1) * peers, :] = jnp.broadcast_to(
            rows[t : t + 1, :], (peers, rows.shape[1])
        )


def pack_kernel(
    meta_ref, w1_ref, w2_ref, w3_ref, w4_ref, dense_ref, b1_ref, b2_ref, b3_ref, pack_ref, bottom_ref
):
    core = meta_ref[2]
    w1 = w1_ref[...]
    lead, tail = w1[:HEAD_ROWS], w1[HEAD_ROWS:]
    padded = jnp.concatenate(
        [tail, jnp.zeros((HEAD_ROWS - tail.shape[0], tail.shape[1]), BF)], axis=0
    )
    pack_ref[0:HEAD_ROWS, :] = jnp.where(core == 0, lead, padded)
    at = HEAD_ROWS
    half = w2_ref.shape[0] // 2
    pack_ref[at : at + half, :] = w2_ref[pl.ds(pl.multiple_of(core * half, half), half), :]
    at += half
    half = w3_ref.shape[0] // 2
    quarter = half // 2
    for q in range(2):
        pack_ref[at : at + quarter, q * 128 : (q + 1) * 128] = w3_ref[
            pl.ds(pl.multiple_of(core * half + q * quarter, quarter), quarter), :
        ]
    at += quarter
    half = w4_ref.shape[1] // 2
    pack_ref[at : at + w4_ref.shape[0], :] = w4_ref[:, pl.ds(pl.multiple_of(core * half, half), half)]
    lower = relu(mm(dense_ref[...], b1_ref[...])).astype(BF)
    middle = relu(mm(lower, b2_ref[...])).astype(BF)
    bottom_ref[...] = relu(mm(middle, b3_ref[...]))


def lookup_kernel(meta_ref, idx_ref, own_ref, other_ref, out_ref, code_ref, lo_ref, count_ref):
    peers, width = idx_ref.shape
    samples = width // HOT
    span = own_ref.shape[0]
    held = 2 * span
    his = held // LO
    bags = GROUP * samples
    per_chunk = 256 // bags
    z, core = meta_ref[1], meta_ref[2]
    rel = idx_ref[...] - z * held
    valid = (rel >= 0) & (rel < held)
    rel = rel ^ (core * span)
    row = lax.broadcasted_iota(jnp.int32, (peers, width), 0)
    lane = lax.broadcasted_iota(jnp.int32, (peers, width), 1)
    bag = (row % GROUP) * samples + lane % samples
    code_ref[...] = jnp.where(valid, (rel // LO) * bags + bag, -1)
    lo_ref[...] = rel % LO
    entries = GROUP * width
    code_rows = lax.broadcasted_iota(jnp.int32, (his * bags, entries), 0)
    lo_rows = lax.broadcasted_iota(jnp.int32, (LO, entries), 0)

    def spread(ref, first):
        return jnp.concatenate([ref[pl.ds(first + k, 1), :] for k in range(GROUP)], axis=1)

    @pl.loop(0, peers // (GROUP * per_chunk))
    def _(chunk):
        for g in range(per_chunk):
            first = (chunk * per_chunk + g) * GROUP
            left = jnp.where(code_rows == spread(code_ref, first), 1.0, 0.0).astype(BF)
            right = jnp.where(lo_rows == spread(lo_ref, first), 1.0, 0.0).astype(BF)
            counts = mm_t(left, right).astype(BF)
            for hi in range(his):
                count_ref[g * bags : (g + 1) * bags, hi * LO : (hi + 1) * LO] = counts[
                    hi * bags : (hi + 1) * bags
                ]
        total = mm(count_ref[:, :span], own_ref[...]) + mm(count_ref[:, span:], other_ref[...])
        rows = per_chunk * bags
        out_ref[pl.ds(pl.multiple_of(chunk * rows, rows), rows), :] = total


def top_kernel(meta_ref, bags_ref, bottom_ref, w1_ref, w2_ref, w3_ref, w4_ref, last_ref, *rest):
    near, far = rest[0:3], rest[3:6]
    out_ref, in_ref, a1_ref, a2_ref, a3_ref = rest[6:]
    core, x = meta_ref[2], meta_ref[3]
    reps = 1 + len(near)
    peers = bags_ref.shape[0] // TAB
    bottom = bottom_ref[...]
    vectors = [bottom]
    for t in range(TAB):
        total = bags_ref[t * peers]
        for k in range(1, peers):
            total = total + bags_ref[t * peers + k]
        vectors.append(total)
    lane = lax.broadcasted_iota(jnp.int32, bottom.shape, 1)
    pairs = jnp.zeros(bottom.shape, F32)
    at = 0
    for i in range(TAB + 1):
        for j in range(i + 1, TAB + 1):
            dots = jnp.sum(vectors[i] * vectors[j], axis=1, keepdims=True)
            pairs = jnp.where(lane == at, dots, pairs)
            at += 1
    in_ref[0] = bottom.astype(BF)
    in_ref[1] = pairs.astype(BF)
    owners = [lax.rem(x - k + reps, reps) for k in range(reps)]
    halves = (core, 1 - core)

    def sides(k):
        return zip(halves, (near[k - 1], far[k - 1]))

    tail = w1_ref.shape[0] - HEAD_ROWS
    for k in range(reps):
        if k == 0:
            y = mm(in_ref[0], w1_ref[0:HEAD_ROWS, :]) + mm(in_ref[1][:, :tail], w1_ref[HEAD_ROWS:, :])
        else:
            y = sum(mm(in_ref[h], w[0:HEAD_ROWS, :]) for h, w in sides(k))
        a1_ref[owners[k]] = relu(y).astype(BF)
    base = HEAD_ROWS
    for k in range(reps):
        if k == 0:
            y = sum(mm(a1_ref[q], w2_ref[q * 256 : (q + 1) * 256, :]) for q in range(4))
        else:
            y = sum(
                mm(a1_ref[2 * h + q], w[base + q * 256 : base + (q + 1) * 256, :])
                for h, w in sides(k)
                for q in range(2)
            )
        a2_ref[owners[k]] = relu(y).astype(BF)
    base += 512
    for k in range(reps):
        if k == 0:
            y = sum(mm(a2_ref[q], w3_ref[q * 256 : (q + 1) * 256, :]) for q in range(4))
        else:
            y = sum(
                mm(a2_ref[2 * h + q], w[base : base + 256, q * 128 : (q + 1) * 128])
                for h, w in sides(k)
                for q in range(2)
            )
        a3_ref[owners[k]] = relu(y).astype(BF)
    base += 256
    logit = jnp.zeros(out_ref.shape, F32)
    for k in range(reps):
        if k == 0:
            y = sum(mm_t(a3_ref[q], w4_ref[:, q * 128 : (q + 1) * 128]) for q in range(4))
        else:
            y = sum(
                mm_t(a3_ref[2 * h + q], w[base : base + 64, q * 128 : (q + 1) * 128])
                for h, w in sides(k)
                for q in range(2)
            )
        logit = logit + mm_t(last_ref[owners[k]], relu(y).astype(BF))
    out_ref[...] = logit


def shifted(a, axis, k):
    n = lax.axis_size(axis)
    return lax.ppermute(a, axis, [(i, (i + k) % n) for i in range(n)])


def body(tables, indices, bag_lengths, dense, b1, b2, b3, w1, w2, w3, w4, last):
    samples, width = indices.shape[0], tables.shape[1]
    reps = lax.axis_size(X)
    along_z = lax.axis_size(Z)
    peers = lax.axis_size((Y, Z))
    meta = jnp.stack([lax.axis_index(a) for a in ALL]).astype(jnp.int32)
    rows = pl.pallas_call(
        functools.partial(prepare_kernel, along_z),
        out_shape=jax.ShapeDtypeStruct((peers, HOT * samples), jnp.int32),
        in_specs=[VM] * 2,
        out_specs=VM,
        compiler_params=params(8),
        cost_estimate=cost(1),
        name="prepare",
    )(jnp.transpose(indices, (1, 2, 0)), jnp.transpose(bag_lengths))
    rows, tables, meta = lax.optimization_barrier((rows, tables, meta))
    wanted = lax.all_to_all(rows, (Y, Z), 0, 0, tiled=True)
    other = shifted(tables, C, 1)
    w4t = jnp.transpose(w4)
    pack_rows = HEAD_ROWS + w2.shape[0] // 2 + w3.shape[0] // 4 + w4t.shape[0]
    pack, bottom = pl.pallas_call(
        pack_kernel,
        out_shape=(
            jax.ShapeDtypeStruct((pack_rows, w2.shape[1]), BF),
            jax.ShapeDtypeStruct((samples, width), F32),
        ),
        in_specs=[SM] + [VM] * 8,
        out_specs=(VM, VM),
        compiler_params=params(12),
        cost_estimate=cost(3),
        name="pack",
    )(meta, w1, w2, w3, w4t, dense, b1, b2, b3)
    near = [shifted(pack, X, k) for k in range(1, reps)]
    partial_bags = pl.pallas_call(
        lookup_kernel,
        out_shape=jax.ShapeDtypeStruct((peers * samples, width), F32),
        in_specs=[SM] + [VM] * 3,
        out_specs=VM,
        scratch_shapes=[
            pltpu.VMEM(wanted.shape, jnp.int32),
            pltpu.VMEM(wanted.shape, jnp.int32),
            pltpu.VMEM((256, 2 * tables.shape[0]), BF),
        ],
        compiler_params=params(24),
        cost_estimate=cost(40),
        name="lookup",
    )(meta, wanted, tables, other)
    partial_bags, *near = lax.optimization_barrier((partial_bags, *near))
    far = [shifted(p, C, 1) for p in near]
    bags = lax.all_to_all(
        partial_bags.reshape(peers, samples, width), (Y, Z), 0, 0, tiled=True
    )
    logit = pl.pallas_call(
        top_kernel,
        out_shape=jax.ShapeDtypeStruct((1, samples), F32),
        in_specs=[SM] + [VM] * 13,
        out_specs=VM,
        scratch_shapes=[
            pltpu.VMEM((2, samples, width), BF),
            pltpu.VMEM((reps, samples, w1.shape[1]), BF),
            pltpu.VMEM((reps, samples, w2.shape[1]), BF),
            pltpu.VMEM((reps, samples, w3.shape[1]), BF),
        ],
        compiler_params=params(16),
        cost_estimate=cost(5),
        name="top",
    )(meta, bags, bottom, w1, w2, w3, w4t, last.reshape(reps, 1, -1), *near, *far)
    return logit.reshape(samples)


def solution(mesh):
    torus = Mesh(mesh.devices.reshape(8, 8, 2, mesh.shape["rep"]), ALL)
    in_specs = (
        P((Y, Z, C), None),
        P(ALL, None, None),
        P(ALL, None),
        P(ALL, None),
        P(),
        P(),
        P(),
        P(None, X),
        P(None, X),
        P(None, X),
        P(None, X),
        P(),
    )
    return jax.shard_map(body, mesh=torus, in_specs=in_specs, out_specs=P(ALL), check_vma=False)
```

```python
import functools

import jax
import jax.numpy as jnp
from jax import lax
from jax.experimental import pallas as pl
from jax.experimental.pallas import tpu as pltpu
from jax.sharding import Mesh
from jax.sharding import PartitionSpec as P

TAB = 8
HOT = 8
Y, Z, C, X = "y", "z", "c", "x"
ALL = (Y, Z, C, X)
LO = 256
HEAD_ROWS = 128
BF = jnp.bfloat16
F8 = jnp.float8_e4m3fn
F32 = jnp.float32
VM = pl.BlockSpec(memory_space=pltpu.VMEM)
SM = pl.BlockSpec(memory_space=pltpu.SMEM)
LANES = (((1,), (1,)), ((), ()))


def mm(a, b):
    return jnp.dot(a, b, preferred_element_type=F32)


def mm_t(a, b):
    return lax.dot_general(a, b, LANES, preferred_element_type=F32)


def relu(a):
    return jnp.maximum(a, 0.0)


def cost(micros):
    return pl.CostEstimate(flops=int(micros * 1.0e9), bytes_accessed=1 << 20, transcendentals=0)


def params(mib):
    return pltpu.CompilerParams(vmem_limit_bytes=mib << 20)


def prepare_kernel(peers, idx_ref, len_ref, out_ref):
    lens = len_ref[...]
    parts = [jnp.where(lens > h, idx_ref[:, h, :], -1) for h in range(HOT)]
    rows = jnp.concatenate(parts, axis=1)
    for t in range(TAB):
        out_ref[t * peers : (t + 1) * peers, :] = jnp.broadcast_to(
            rows[t : t + 1, :], (peers, rows.shape[1])
        )


def pack_kernel(
    meta_ref, w1_ref, w2_ref, w3_ref, w4_ref, dense_ref, b1_ref, b2_ref, b3_ref, pack_ref, half_ref, bottom_ref
):
    core = meta_ref[2]
    tail = w1_ref[HEAD_ROWS:, :]
    pack_ref[0, 0:HEAD_ROWS, :] = w1_ref[0:HEAD_ROWS, :]
    pack_ref[1, 0:HEAD_ROWS, :] = jnp.concatenate(
        [tail, jnp.zeros((HEAD_ROWS - tail.shape[0], tail.shape[1]), BF)], axis=0
    )
    for h in range(2):
        at = HEAD_ROWS
        half = w2_ref.shape[0] // 2
        pack_ref[h, at : at + half, :] = w2_ref[h * half : (h + 1) * half, :]
        at += half
        half = w3_ref.shape[0] // 2
        quarter = half // 2
        for q in range(2):
            first = h * half + q * quarter
            pack_ref[h, at : at + quarter, q * 128 : (q + 1) * 128] = w3_ref[first : first + quarter, :]
        at += quarter
        half = w4_ref.shape[1] // 2
        pack_ref[h, at : at + w4_ref.shape[0], :] = w4_ref[:, h * half : (h + 1) * half]
    half_ref[...] = pack_ref[core]
    lower = relu(mm(dense_ref[...], b1_ref[...])).astype(BF)
    middle = relu(mm(lower, b2_ref[...])).astype(BF)
    bottom_ref[...] = relu(mm(middle, b3_ref[...]))


def lookup_kernel(meta_ref, idx_ref, own_ref, other_ref, out_ref, code_ref, lo_ref, count_ref):
    peers, width = idx_ref.shape
    bags = width // HOT
    span = own_ref.shape[0]
    held = 2 * span
    his = held // LO
    rows = count_ref.shape[0]
    per_chunk = rows // bags
    z, core = meta_ref[1], meta_ref[2]
    rel = idx_ref[...] - z * held
    valid = (rel >= 0) & (rel < held)
    rel = rel ^ (core * span)
    bag = lax.broadcasted_iota(jnp.int32, (peers, width), 1) % bags
    code_ref[...] = jnp.where(valid, (rel // LO) * bags + bag, -1)
    lo_ref[...] = rel % LO
    one, zero = jnp.ones((), BF), jnp.zeros((), BF)

    def one_hot(height, ref, peer):
        ids = lax.broadcasted_iota(jnp.int16, (height, width), 0)
        return jnp.where(ids == ref[pl.ds(peer, 1), :].astype(jnp.int16), one, zero).astype(F8)

    @pl.loop(0, peers // per_chunk)
    def _(chunk):
        for g in range(per_chunk):
            peer = chunk * per_chunk + g
            left = one_hot(his * bags, code_ref, peer)
            counts = mm_t(left, one_hot(LO, lo_ref, peer)).astype(BF)
            for hi in range(his):
                count_ref[g * bags : (g + 1) * bags, hi * LO : (hi + 1) * LO] = counts[
                    hi * bags : (hi + 1) * bags
                ]
        total = mm(count_ref[:, :span], own_ref[...]) + mm(count_ref[:, span:], other_ref[...])
        out_ref[pl.ds(pl.multiple_of(chunk * rows, rows), rows), :] = total


def top_kernel(
    meta_ref, bags_ref, bottom_ref, last_ref, own_ref, side_ref, mirror_ref, near_ref, far_ref,
    out_ref, in_ref, a1_ref, a2_ref, a3_ref,
):
    core, x = meta_ref[2], meta_ref[3]
    reps = last_ref.shape[0]
    peers = bags_ref.shape[0] // TAB
    bottom = bottom_ref[...]
    vectors = [bottom]
    for t in range(TAB):
        total = bags_ref[t * peers]
        for k in range(1, peers):
            total = total + bags_ref[t * peers + k]
        vectors.append(total)
    lane = lax.broadcasted_iota(jnp.int32, bottom.shape, 1)
    pairs = jnp.zeros(bottom.shape, F32)
    at = 0
    for i in range(TAB + 1):
        for j in range(i + 1, TAB + 1):
            dots = jnp.sum(vectors[i] * vectors[j], axis=1, keepdims=True)
            pairs = jnp.where(lane == at, dots, pairs)
            at += 1
    in_ref[0] = bottom.astype(BF)
    in_ref[1] = pairs.astype(BF)

    def whole(ref):
        return [(h, ref.at[h]) for h in range(2)]

    before, after = lax.rem(x + reps - 1, reps), lax.rem(x + 1, reps)
    shards = (
        (x, whole(own_ref)),
        (jnp.where(core == 0, before, after), whole(side_ref)),
        (jnp.where(core == 0, after, before), whole(mirror_ref)),
        (lax.rem(x + 2, reps), [(core, near_ref), (1 - core, far_ref)]),
    )
    for owner, halves in shards:
        y = sum(mm(in_ref[h], w[0:HEAD_ROWS, :]) for h, w in halves)
        a1_ref[owner] = relu(y).astype(BF)
    base = HEAD_ROWS
    for owner, halves in shards:
        y = sum(
            mm(a1_ref[2 * h + q], w[base + q * 256 : base + (q + 1) * 256, :])
            for h, w in halves
            for q in range(2)
        )
        a2_ref[owner] = relu(y).astype(BF)
    base += 512
    for owner, halves in shards:
        y = sum(
            mm(a2_ref[2 * h + q], w[base : base + 256, q * 128 : (q + 1) * 128])
            for h, w in halves
            for q in range(2)
        )
        a3_ref[owner] = relu(y).astype(BF)
    base += 256
    logit = jnp.zeros(out_ref.shape, F32)
    for owner, halves in shards:
        y = sum(
            mm_t(a3_ref[2 * h + q], w[base : base + 64, q * 128 : (q + 1) * 128])
            for h, w in halves
            for q in range(2)
        )
        logit = logit + mm_t(last_ref[owner], relu(y).astype(BF))
    out_ref[...] = logit


def shifted(a, axis, k):
    n = lax.axis_size(axis)
    return lax.ppermute(a, axis, [(i, (i + k) % n) for i in range(n)])


def body(tables, indices, bag_lengths, dense, b1, b2, b3, w1, w2, w3, w4, last):
    samples, width = indices.shape[0], tables.shape[1]
    reps = lax.axis_size(X)
    along_z = lax.axis_size(Z)
    peers = lax.axis_size((Y, Z))
    meta = jnp.stack([lax.axis_index(a) for a in ALL]).astype(jnp.int32)
    rows = pl.pallas_call(
        functools.partial(prepare_kernel, along_z),
        out_shape=jax.ShapeDtypeStruct((peers, HOT * samples), jnp.int32),
        in_specs=[VM] * 2,
        out_specs=VM,
        compiler_params=params(8),
        cost_estimate=cost(1),
        name="prepare",
    )(jnp.transpose(indices, (1, 2, 0)), jnp.transpose(bag_lengths))
    rows, tables, meta = lax.optimization_barrier((rows, tables, meta))
    wanted = lax.all_to_all(rows, (Y, Z), 0, 0, tiled=True)
    other = shifted(tables, C, 1)
    w4t = jnp.transpose(w4)
    pack_rows = HEAD_ROWS + w2.shape[0] // 2 + w3.shape[0] // 4 + w4t.shape[0]
    pack, half, bottom = pl.pallas_call(
        pack_kernel,
        out_shape=(
            jax.ShapeDtypeStruct((2, pack_rows, w2.shape[1]), BF),
            jax.ShapeDtypeStruct((pack_rows, w2.shape[1]), BF),
            jax.ShapeDtypeStruct((samples, width), F32),
        ),
        in_specs=[SM] + [VM] * 8,
        out_specs=(VM, VM, VM),
        compiler_params=params(12),
        cost_estimate=cost(3),
        name="pack",
    )(meta, w1, w2, w3, w4t, dense, b1, b2, b3)
    sides = [(i, (i + 1) % reps) for i in range(reps)]
    sides += [(reps + i, reps + (i - 1) % reps) for i in range(reps)]
    side = lax.ppermute(pack, (C, X), sides)
    near = shifted(half, X, 2)
    partial_bags = pl.pallas_call(
        lookup_kernel,
        out_shape=jax.ShapeDtypeStruct((peers * samples, width), F32),
        in_specs=[SM] + [VM] * 3,
        out_specs=VM,
        scratch_shapes=[
            pltpu.VMEM(wanted.shape, jnp.int32),
            pltpu.VMEM(wanted.shape, jnp.int32),
            pltpu.VMEM((512, 2 * tables.shape[0]), BF),
        ],
        compiler_params=params(24),
        cost_estimate=cost(40),
        name="lookup",
    )(meta, wanted, tables, other)
    partial_bags, side = lax.optimization_barrier((partial_bags, side))
    mirror = shifted(side, C, 1)
    far = shifted(near, C, 1)
    bags = lax.all_to_all(
        partial_bags.reshape(peers, samples, width), (Y, Z), 0, 0, tiled=True
    )
    logit = pl.pallas_call(
        top_kernel,
        out_shape=jax.ShapeDtypeStruct((1, samples), F32),
        in_specs=[SM] + [VM] * 8,
        out_specs=VM,
        scratch_shapes=[
            pltpu.VMEM((2, samples, width), BF),
            pltpu.VMEM((reps, samples, w1.shape[1]), BF),
            pltpu.VMEM((reps, samples, w2.shape[1]), BF),
            pltpu.VMEM((reps, samples, w3.shape[1]), BF),
        ],
        compiler_params=params(16),
        cost_estimate=cost(5),
        name="top",
    )(meta, bags, bottom, last.reshape(reps, 1, -1), pack, side, mirror, near, far)
    return logit.reshape(samples)


def solution(mesh):
    torus = Mesh(mesh.devices.reshape(8, 8, 2, mesh.shape["rep"]), ALL)
    in_specs = (
        P((Y, Z, C), None),
        P(ALL, None, None),
        P(ALL, None),
        P(ALL, None),
        P(),
        P(),
        P(),
        P(None, X),
        P(None, X),
        P(None, X),
        P(None, X),
        P(),
    )
    return jax.shard_map(body, mesh=torus, in_specs=in_specs, out_specs=P(ALL), check_vma=False)
```

```python
import functools

import jax
import jax.numpy as jnp
from jax import lax
from jax.experimental import pallas as pl
from jax.experimental.pallas import tpu as pltpu
from jax.sharding import Mesh
from jax.sharding import PartitionSpec as P

TAB = 8
HOT = 8
Y, Z, C, X = "y", "z", "c", "x"
ALL = (Y, Z, C, X)
LO = 256
HEAD_ROWS = 128
BF = jnp.bfloat16
F8 = jnp.float8_e4m3fn
F32 = jnp.float32
VM = pl.BlockSpec(memory_space=pltpu.VMEM)
SM = pl.BlockSpec(memory_space=pltpu.SMEM)
LANES = (((1,), (1,)), ((), ()))


def mm(a, b):
    return jnp.dot(a, b, preferred_element_type=F32)


def mm_t(a, b):
    return lax.dot_general(a, b, LANES, preferred_element_type=F32)


def relu(a):
    return jnp.maximum(a, 0.0)


def cost(micros):
    return pl.CostEstimate(flops=int(micros * 1.0e9), bytes_accessed=1 << 20, transcendentals=0)


def params(mib):
    return pltpu.CompilerParams(vmem_limit_bytes=mib << 20)


def prepare_kernel(peers, idx_ref, len_ref, out_ref):
    lens = len_ref[...]
    parts = [jnp.where(lens > h, idx_ref[:, h, :], -1) for h in range(HOT)]
    rows = jnp.concatenate(parts, axis=1)
    for t in range(TAB):
        out_ref[t * peers : (t + 1) * peers, :] = jnp.broadcast_to(
            rows[t : t + 1, :], (peers, rows.shape[1])
        )


def pack_kernel(
    meta_ref, w1_ref, w2_ref, w3_ref, w4_ref, dense_ref, b1_ref, b2_ref, b3_ref, pack_ref, half_ref, bottom_ref
):
    core = meta_ref[2]
    tail = w1_ref[HEAD_ROWS:, :]
    pack_ref[0, 0:HEAD_ROWS, :] = w1_ref[0:HEAD_ROWS, :]
    pack_ref[1, 0:HEAD_ROWS, :] = jnp.concatenate(
        [tail, jnp.zeros((HEAD_ROWS - tail.shape[0], tail.shape[1]), BF)], axis=0
    )
    for h in range(2):
        at = HEAD_ROWS
        half = w2_ref.shape[0] // 2
        pack_ref[h, at : at + half, :] = w2_ref[h * half : (h + 1) * half, :]
        at += half
        half = w3_ref.shape[0] // 2
        quarter = half // 2
        for q in range(2):
            first = h * half + q * quarter
            pack_ref[h, at : at + quarter, q * 128 : (q + 1) * 128] = w3_ref[first : first + quarter, :]
        at += quarter
        half = w4_ref.shape[1] // 2
        pack_ref[h, at : at + w4_ref.shape[0], :] = w4_ref[:, h * half : (h + 1) * half]
    half_ref[...] = pack_ref[core]
    lower = relu(mm(dense_ref[...], b1_ref[...])).astype(BF)
    middle = relu(mm(lower, b2_ref[...])).astype(BF)
    bottom_ref[...] = relu(mm(middle, b3_ref[...]))


def lookup_kernel(meta_ref, idx_ref, own_ref, other_ref, out_ref, code_ref, lo_ref, count_ref):
    peers, width = idx_ref.shape
    bags = width // HOT
    span = own_ref.shape[0]
    held = 2 * span
    his = held // LO
    rows = count_ref.shape[0]
    per_chunk = rows // bags
    z, core = meta_ref[1], meta_ref[2]
    rel = idx_ref[...] - z * held
    valid = (rel >= 0) & (rel < held)
    rel = rel ^ (core * span)
    bag = lax.broadcasted_iota(jnp.int32, (peers, width), 1) % bags
    code_ref[...] = jnp.where(valid, (rel // LO) * bags + bag, -1)
    lo_ref[...] = rel % LO
    one, zero = jnp.ones((), BF), jnp.zeros((), BF)

    def one_hot(height, ref, peer):
        ids = lax.broadcasted_iota(jnp.int16, (height, width), 0)
        return jnp.where(ids == ref[pl.ds(peer, 1), :].astype(jnp.int16), one, zero).astype(F8)

    @pl.loop(0, peers // per_chunk)
    def _(chunk):
        for g in range(per_chunk):
            peer = chunk * per_chunk + g
            left = one_hot(his * bags, code_ref, peer)
            counts = mm_t(left, one_hot(LO, lo_ref, peer)).astype(BF)
            for hi in range(his):
                count_ref[g * bags : (g + 1) * bags, hi * LO : (hi + 1) * LO] = counts[
                    hi * bags : (hi + 1) * bags
                ]
        total = mm(count_ref[:, :span], own_ref[...]) + mm(count_ref[:, span:], other_ref[...])
        out_ref[pl.ds(pl.multiple_of(chunk * rows, rows), rows), :] = total


def top_kernel(
    meta_ref, bags_ref, bottom_ref, last_ref, own_ref, side_ref, mirror_ref, near_ref, far_ref,
    out_ref, in_ref, a1_ref, a2_ref, a3_ref,
):
    core, x = meta_ref[2], meta_ref[3]
    reps = last_ref.shape[0]
    peers = bags_ref.shape[0] // TAB
    bottom = bottom_ref[...]
    vectors = [bottom]
    for t in range(TAB):
        total = bags_ref[t * peers]
        for k in range(1, peers):
            total = total + bags_ref[t * peers + k]
        vectors.append(total)
    lane = lax.broadcasted_iota(jnp.int32, bottom.shape, 1)
    pairs = jnp.zeros(bottom.shape, F32)
    at = 0
    for i in range(TAB + 1):
        for j in range(i + 1, TAB + 1):
            dots = jnp.sum(vectors[i] * vectors[j], axis=1, keepdims=True)
            pairs = jnp.where(lane == at, dots, pairs)
            at += 1
    in_ref[0] = bottom.astype(BF)
    in_ref[1] = pairs.astype(BF)

    def whole(ref):
        return [(h, ref.at[h]) for h in range(2)]

    before, after = lax.rem(x + reps - 1, reps), lax.rem(x + 1, reps)
    shards = (
        (x, whole(own_ref)),
        (jnp.where(core == 0, before, after), whole(side_ref)),
        (jnp.where(core == 0, after, before), whole(mirror_ref)),
        (lax.rem(x + 2, reps), [(core, near_ref), (1 - core, far_ref)]),
    )
    for owner, halves in shards:
        y = sum(mm(in_ref[h], w[0:HEAD_ROWS, :]) for h, w in halves)
        a1_ref[owner] = relu(y).astype(BF)
    base = HEAD_ROWS
    for owner, halves in shards:
        y = sum(
            mm(a1_ref[2 * h + q], w[base + q * 256 : base + (q + 1) * 256, :])
            for h, w in halves
            for q in range(2)
        )
        a2_ref[owner] = relu(y).astype(BF)
    base += 512
    for owner, halves in shards:
        y = sum(
            mm(a2_ref[2 * h + q], w[base : base + 256, q * 128 : (q + 1) * 128])
            for h, w in halves
            for q in range(2)
        )
        a3_ref[owner] = relu(y).astype(BF)
    base += 256
    logit = jnp.zeros(out_ref.shape, F32)
    for owner, halves in shards:
        y = sum(
            mm_t(a3_ref[2 * h + q], w[base : base + 64, q * 128 : (q + 1) * 128])
            for h, w in halves
            for q in range(2)
        )
        logit = logit + mm_t(last_ref[owner], relu(y).astype(BF))
    out_ref[...] = logit


def shifted(a, axis, k):
    n = lax.axis_size(axis)
    return lax.ppermute(a, axis, [(i, (i + k) % n) for i in range(n)])


def hold_kernel(in_ref, out_ref):
    pass


def held(a, micros, space):
    spec = pl.BlockSpec(memory_space=space)
    return pl.pallas_call(
        hold_kernel,
        out_shape=jax.ShapeDtypeStruct(a.shape, a.dtype),
        in_specs=[spec],
        out_specs=spec,
        input_output_aliases={0: 0},
        compiler_params=params(4),
        cost_estimate=cost(micros),
        name="held",
    )(a)


def body(tables, indices, bag_lengths, dense, b1, b2, b3, w1, w2, w3, w4, last):
    samples, width = indices.shape[0], tables.shape[1]
    reps = lax.axis_size(X)
    along_z = lax.axis_size(Z)
    peers = lax.axis_size((Y, Z))
    meta = jnp.stack([lax.axis_index(a) for a in ALL]).astype(jnp.int32)
    rows = pl.pallas_call(
        functools.partial(prepare_kernel, along_z),
        out_shape=jax.ShapeDtypeStruct((peers, HOT * samples), jnp.int32),
        in_specs=[VM] * 2,
        out_specs=VM,
        compiler_params=params(8),
        cost_estimate=cost(1),
        name="prepare",
    )(jnp.transpose(indices, (1, 2, 0)), jnp.transpose(bag_lengths))
    rows, tables, meta = lax.optimization_barrier((rows, tables, meta))
    wanted = lax.all_to_all(rows, (Y, Z), 0, 0, tiled=True)
    other = shifted(tables, C, 1)
    w4t = jnp.transpose(w4)
    pack_rows = HEAD_ROWS + w2.shape[0] // 2 + w3.shape[0] // 4 + w4t.shape[0]
    pack, half, bottom = pl.pallas_call(
        pack_kernel,
        out_shape=(
            jax.ShapeDtypeStruct((2, pack_rows, w2.shape[1]), BF),
            jax.ShapeDtypeStruct((pack_rows, w2.shape[1]), BF),
            jax.ShapeDtypeStruct((samples, width), F32),
        ),
        in_specs=[SM] + [VM] * 8,
        out_specs=(VM, VM, VM),
        compiler_params=params(10),
        cost_estimate=cost(3),
        name="pack",
    )(meta, w1, w2, w3, w4t, dense, b1, b2, b3)
    sides = [(i, (i + 1) % reps) for i in range(reps)]
    sides += [(reps + i, reps + (i - 1) % reps) for i in range(reps)]
    side = lax.ppermute(pack, (C, X), sides)
    near = shifted(half, X, 2)
    partial_bags = pl.pallas_call(
        lookup_kernel,
        out_shape=jax.ShapeDtypeStruct((peers * samples, width), F32),
        in_specs=[SM] + [VM] * 3,
        out_specs=VM,
        scratch_shapes=[
            pltpu.VMEM(wanted.shape, jnp.int32),
            pltpu.VMEM(wanted.shape, jnp.int32),
            pltpu.VMEM((512, 2 * tables.shape[0]), BF),
        ],
        compiler_params=params(14),
        cost_estimate=cost(40),
        name="lookup",
    )(meta, wanted, tables, other)
    side, near = held(side, 60, pltpu.VMEM), held(near, 60, pl.ANY)
    mirror = shifted(side, C, 1)
    far = shifted(near, C, 1)
    bags = lax.all_to_all(
        partial_bags.reshape(peers, samples, width), (Y, Z), 0, 0, tiled=True
    )
    logit = pl.pallas_call(
        top_kernel,
        out_shape=jax.ShapeDtypeStruct((1, samples), F32),
        in_specs=[SM] + [VM] * 8,
        out_specs=VM,
        scratch_shapes=[
            pltpu.VMEM((2, samples, width), BF),
            pltpu.VMEM((reps, samples, w1.shape[1]), BF),
            pltpu.VMEM((reps, samples, w2.shape[1]), BF),
            pltpu.VMEM((reps, samples, w3.shape[1]), BF),
        ],
        compiler_params=params(10),
        cost_estimate=cost(5),
        name="top",
    )(meta, bags, bottom, last.reshape(reps, 1, -1), pack, side, mirror, near, far)
    return logit.reshape(samples)


def solution(mesh):
    torus = Mesh(mesh.devices.reshape(8, 8, 2, mesh.shape["rep"]), ALL)
    in_specs = (
        P((Y, Z, C), None),
        P(ALL, None, None),
        P(ALL, None),
        P(ALL, None),
        P(),
        P(),
        P(),
        P(None, X),
        P(None, X),
        P(None, X),
        P(None, X),
        P(),
    )
    return jax.shard_map(body, mesh=torus, in_specs=in_specs, out_specs=P(ALL), check_vma=False)
```

```python
import functools

import jax
import jax.numpy as jnp
from jax import lax
from jax.experimental import pallas as pl
from jax.experimental.pallas import tpu as pltpu
from jax.sharding import Mesh
from jax.sharding import PartitionSpec as P

TAB = 8
HOT = 8
Y, Z, N, C, X = "y", "z", "n", "c", "x"
ALL = (Y, Z, N, C, X)
LO = 256
HEAD_ROWS = 128
BF = jnp.bfloat16
F8 = jnp.float8_e4m3fn
F32 = jnp.float32
VM = pl.BlockSpec(memory_space=pltpu.VMEM)
SM = pl.BlockSpec(memory_space=pltpu.SMEM)
LANES = (((1,), (1,)), ((), ()))


def mm(a, b):
    return jnp.dot(a, b, preferred_element_type=F32)


def mm_t(a, b):
    return lax.dot_general(a, b, LANES, preferred_element_type=F32)


def relu(a):
    return jnp.maximum(a, 0.0)


def cost(micros):
    return pl.CostEstimate(flops=int(micros * 1.0e9), bytes_accessed=1 << 20, transcendentals=0)


def params(mib):
    return pltpu.CompilerParams(vmem_limit_bytes=mib << 20)


def prepare_kernel(peers, idx_hbm, len_hbm, out_ref, idx_ref, len_ref, sem):
    copies = [
        pltpu.make_async_copy(idx_hbm, idx_ref, sem.at[0]),
        pltpu.make_async_copy(len_hbm, len_ref, sem.at[1]),
    ]
    for copy in copies:
        copy.start()
    for copy in copies:
        copy.wait()
    lens = len_ref[...]
    parts = [jnp.where(lens > h, idx_ref[:, h, :], -1) for h in range(HOT)]
    rows = jnp.concatenate(parts, axis=1)
    for t in range(TAB):
        out_ref[t * peers : (t + 1) * peers, :] = jnp.broadcast_to(
            rows[t : t + 1, :], (peers, rows.shape[1])
        )


def pack_kernel(
    meta_ref, w1_ref, w2_ref, w3_ref, w4_ref, dense_ref, b1_ref, b2_ref, b3_ref, pack_ref, half_ref, bottom_ref
):
    core = meta_ref[3]
    tail = w1_ref[HEAD_ROWS:, :]
    pack_ref[0, 0:HEAD_ROWS, :] = w1_ref[0:HEAD_ROWS, :]
    pack_ref[1, 0:HEAD_ROWS, :] = jnp.concatenate(
        [tail, jnp.zeros((HEAD_ROWS - tail.shape[0], tail.shape[1]), BF)], axis=0
    )
    for h in range(2):
        at = HEAD_ROWS
        half = w2_ref.shape[0] // 2
        pack_ref[h, at : at + half, :] = w2_ref[h * half : (h + 1) * half, :]
        at += half
        half = w3_ref.shape[0] // 2
        quarter = half // 2
        for q in range(2):
            first = h * half + q * quarter
            pack_ref[h, at : at + quarter, q * 128 : (q + 1) * 128] = w3_ref[first : first + quarter, :]
        at += quarter
        half = w4_ref.shape[1] // 2
        pack_ref[h, at : at + w4_ref.shape[0], :] = w4_ref[:, h * half : (h + 1) * half]
    half_ref[...] = pack_ref[core]
    lower = relu(mm(dense_ref[...], b1_ref[...])).astype(BF)
    middle = relu(mm(lower, b2_ref[...])).astype(BF)
    bottom_ref[...] = relu(mm(middle, b3_ref[...]))


def lookup_kernel(meta_ref, idx_ref, same_ref, other_ref, out_ref, code_ref, lo_ref, count_ref):
    peers, width = idx_ref.shape
    bags = width // HOT
    near, span = same_ref.shape[0], same_ref.shape[1]
    held = 2 * near * span
    his = held // LO
    rows = count_ref.shape[0]
    per_chunk = rows // bags
    z, n, core = meta_ref[1], meta_ref[2], meta_ref[3]
    rel = idx_ref[...] - z * held
    valid = (rel >= 0) & (rel < held)
    rel = rel ^ ((n * 2 + core) * span)
    bag = lax.broadcasted_iota(jnp.int32, (peers, width), 1) % bags
    code_ref[...] = jnp.where(valid, (rel // LO) * bags + bag, -1)
    lo_ref[...] = rel % LO
    one, zero = jnp.ones((), BF), jnp.zeros((), BF)

    def one_hot(height, ref, peer):
        ids = lax.broadcasted_iota(jnp.int16, (height, width), 0)
        return jnp.where(ids == ref[pl.ds(peer, 1), :].astype(jnp.int16), one, zero).astype(F8)

    @pl.loop(0, peers // per_chunk)
    def _(chunk):
        for g in range(per_chunk):
            peer = chunk * per_chunk + g
            left = one_hot(his * bags, code_ref, peer)
            counts = mm_t(left, one_hot(LO, lo_ref, peer)).astype(BF)
            for hi in range(his):
                count_ref[g * bags : (g + 1) * bags, hi * LO : (hi + 1) * LO] = counts[
                    hi * bags : (hi + 1) * bags
                ]
        blocks = [ref[k] for k in range(near) for ref in (same_ref, other_ref)]
        total = sum(mm(count_ref[:, k * span : (k + 1) * span], b) for k, b in enumerate(blocks))
        out_ref[pl.ds(pl.multiple_of(chunk * rows, rows), rows), :] = total


def top_kernel(
    meta_ref, bags_ref, bottom_ref, last_ref, own_ref, side_ref, mirror_ref, near_ref, far_ref,
    out_ref, in_ref, a1_ref, a2_ref, a3_ref,
):
    core, x = meta_ref[3], meta_ref[4]
    reps = last_ref.shape[0]
    peers = bags_ref.shape[0] // TAB
    bottom = bottom_ref[...]
    vectors = [bottom]
    for t in range(TAB):
        total = bags_ref[t * peers]
        for k in range(1, peers):
            total = total + bags_ref[t * peers + k]
        vectors.append(total)
    lane = lax.broadcasted_iota(jnp.int32, bottom.shape, 1)
    pairs = jnp.zeros(bottom.shape, F32)
    at = 0
    for i in range(TAB + 1):
        for j in range(i + 1, TAB + 1):
            dots = jnp.sum(vectors[i] * vectors[j], axis=1, keepdims=True)
            pairs = jnp.where(lane == at, dots, pairs)
            at += 1
    in_ref[0] = bottom.astype(BF)
    in_ref[1] = pairs.astype(BF)

    def whole(ref):
        return [(h, ref.at[h]) for h in range(2)]

    before, after = lax.rem(x + reps - 1, reps), lax.rem(x + 1, reps)
    shards = (
        (x, whole(own_ref)),
        (jnp.where(core == 0, before, after), whole(side_ref)),
        (jnp.where(core == 0, after, before), whole(mirror_ref)),
        (lax.rem(x + 2, reps), [(core, near_ref), (1 - core, far_ref)]),
    )
    for owner, halves in shards:
        y = sum(mm(in_ref[h], w[0:HEAD_ROWS, :]) for h, w in halves)
        a1_ref[owner] = relu(y).astype(BF)
    base = HEAD_ROWS
    for owner, halves in shards:
        y = sum(
            mm(a1_ref[2 * h + q], w[base + q * 256 : base + (q + 1) * 256, :])
            for h, w in halves
            for q in range(2)
        )
        a2_ref[owner] = relu(y).astype(BF)
    base += 512
    for owner, halves in shards:
        y = sum(
            mm(a2_ref[2 * h + q], w[base : base + 256, q * 128 : (q + 1) * 128])
            for h, w in halves
            for q in range(2)
        )
        a3_ref[owner] = relu(y).astype(BF)
    base += 256
    logit = jnp.zeros(out_ref.shape, F32)
    for owner, halves in shards:
        y = sum(
            mm_t(a3_ref[2 * h + q], w[base : base + 64, q * 128 : (q + 1) * 128])
            for h, w in halves
            for q in range(2)
        )
        logit = logit + mm_t(last_ref[owner], relu(y).astype(BF))
    out_ref[...] = logit


def shifted(a, axis, k):
    n = lax.axis_size(axis)
    return lax.ppermute(a, axis, [(i, (i + k) % n) for i in range(n)])


def hold_kernel(in_ref, out_ref):
    pass


def held(a, micros, space):
    spec = pl.BlockSpec(memory_space=space)
    return pl.pallas_call(
        hold_kernel,
        out_shape=jax.ShapeDtypeStruct(a.shape, a.dtype),
        in_specs=[spec],
        out_specs=spec,
        input_output_aliases={0: 0},
        compiler_params=params(4),
        cost_estimate=cost(micros),
        name="held",
    )(a)


def body(tables, indices, bag_lengths, dense, b1, b2, b3, w1, w2, w3, w4, last):
    samples, width = indices.shape[0], tables.shape[1]
    reps = lax.axis_size(X)
    along_z = lax.axis_size(Z)
    pair = lax.axis_size(N)
    peers = lax.axis_size((Y, Z))
    meta = jnp.stack([lax.axis_index(a) for a in ALL]).astype(jnp.int32)
    rows = pl.pallas_call(
        functools.partial(prepare_kernel, along_z),
        out_shape=jax.ShapeDtypeStruct((peers, HOT * samples), jnp.int32),
        in_specs=[pl.BlockSpec(memory_space=pl.ANY)] * 2,
        out_specs=VM,
        scratch_shapes=[
            pltpu.VMEM((TAB, HOT, samples), jnp.int32),
            pltpu.VMEM((TAB, samples), jnp.int32),
            pltpu.SemaphoreType.DMA((2,)),
        ],
        compiler_params=params(8),
        cost_estimate=cost(1),
        name="prepare",
    )(jnp.transpose(indices, (1, 2, 0)), jnp.transpose(bag_lengths))
    rows, tables, meta = lax.optimization_barrier((rows, tables, meta))
    wanted = lax.all_to_all(rows, (Y, Z), 0, 0, tiled=True)
    wanted = held(wanted, 60, pltpu.VMEM)
    beside = shifted(tables, N, 1)
    w4t = jnp.transpose(w4)
    pack_rows = HEAD_ROWS + w2.shape[0] // 2 + w3.shape[0] // 4 + w4t.shape[0]
    pack, half, bottom = pl.pallas_call(
        pack_kernel,
        out_shape=(
            jax.ShapeDtypeStruct((2, pack_rows, w2.shape[1]), BF),
            jax.ShapeDtypeStruct((pack_rows, w2.shape[1]), BF),
            jax.ShapeDtypeStruct((samples, width), F32),
        ),
        in_specs=[SM] + [VM] * 8,
        out_specs=(VM, VM, VM),
        compiler_params=params(10),
        cost_estimate=cost(3),
        name="pack",
    )(meta, w1, w2, w3, w4t, dense, b1, b2, b3)
    sides = [(i, (i + 1) % reps) for i in range(reps)]
    sides += [(reps + i, reps + (i - 1) % reps) for i in range(reps)]
    beside, bottom = lax.optimization_barrier((beside, bottom))
    same = jnp.stack([tables, beside])
    other = shifted(same, C, 1)
    side = lax.ppermute(pack, (C, X), sides)
    near = shifted(half, X, 2)
    partial_bags = pl.pallas_call(
        lookup_kernel,
        out_shape=jax.ShapeDtypeStruct((peers * samples, width), F32),
        in_specs=[SM] + [VM] * 3,
        out_specs=VM,
        scratch_shapes=[
            pltpu.VMEM(wanted.shape, jnp.int32),
            pltpu.VMEM(wanted.shape, jnp.int32),
            pltpu.VMEM((256, 2 * pair * tables.shape[0]), BF),
        ],
        compiler_params=params(14),
        cost_estimate=cost(40),
        name="lookup",
    )(meta, wanted, same, other)
    side, _ = lax.optimization_barrier((side, partial_bags))
    side = held(side, 60, pl.ANY)
    near, _ = lax.optimization_barrier((near, side))
    near = held(near, 60, pl.ANY)
    mirror = shifted(side, C, 1)
    far = shifted(near, C, 1)
    bags = lax.all_to_all(
        partial_bags.reshape(peers, samples, width), (Y, Z), 0, 0, tiled=True
    )
    logit = pl.pallas_call(
        top_kernel,
        out_shape=jax.ShapeDtypeStruct((1, samples), F32),
        in_specs=[SM] + [VM] * 8,
        out_specs=VM,
        scratch_shapes=[
            pltpu.VMEM((2, samples, width), BF),
            pltpu.VMEM((reps, samples, w1.shape[1]), BF),
            pltpu.VMEM((reps, samples, w2.shape[1]), BF),
            pltpu.VMEM((reps, samples, w3.shape[1]), BF),
        ],
        compiler_params=params(10),
        cost_estimate=cost(5),
        name="top",
    )(meta, bags, bottom, last.reshape(reps, 1, -1), pack, side, mirror, near, far)
    return logit.reshape(samples)


def solution(mesh):
    torus = Mesh(mesh.devices.reshape(8, 4, 2, 2, mesh.shape["rep"]), ALL)
    in_specs = (
        P((Y, Z, N, C), None),
        P(ALL, None, None),
        P(ALL, None),
        P(ALL, None),
        P(),
        P(),
        P(),
        P(None, X),
        P(None, X),
        P(None, X),
        P(None, X),
        P(),
    )
    return jax.shard_map(body, mesh=torus, in_specs=in_specs, out_specs=P(ALL), check_vma=False)
```

```python
import functools

import jax
import jax.numpy as jnp
from jax import lax
from jax.experimental import pallas as pl
from jax.experimental.pallas import tpu as pltpu
from jax.sharding import Mesh
from jax.sharding import PartitionSpec as P

TAB = 8
HOT = 8
Y, Z, C, X = "y", "z", "c", "x"
ALL = (Y, Z, C, X)
LO = 256
HEAD_ROWS = 128
BF = jnp.bfloat16
F8 = jnp.float8_e4m3fn
F32 = jnp.float32
VM = pl.BlockSpec(memory_space=pltpu.VMEM)
SM = pl.BlockSpec(memory_space=pltpu.SMEM)
LANES = (((1,), (1,)), ((), ()))


def mm(a, b):
    return jnp.dot(a, b, preferred_element_type=F32)


def mm_t(a, b):
    return lax.dot_general(a, b, LANES, preferred_element_type=F32)


def relu(a):
    return jnp.maximum(a, 0.0)


def cost(micros):
    return pl.CostEstimate(flops=int(micros * 1.0e9), bytes_accessed=1 << 20, transcendentals=0)


def params(mib):
    return pltpu.CompilerParams(vmem_limit_bytes=mib << 20)


def prepare_kernel(peers, idx_hbm, len_hbm, out_ref, idx_ref, len_ref, sem):
    copies = [
        pltpu.make_async_copy(idx_hbm, idx_ref, sem.at[0]),
        pltpu.make_async_copy(len_hbm, len_ref, sem.at[1]),
    ]
    for copy in copies:
        copy.start()
    for copy in copies:
        copy.wait()
    lens = len_ref[...]
    parts = [jnp.where(lens > h, idx_ref[:, h, :], -1) for h in range(HOT)]
    rows = jnp.concatenate(parts, axis=1)
    for t in range(TAB):
        out_ref[t * peers : (t + 1) * peers, :] = jnp.broadcast_to(
            rows[t : t + 1, :], (peers, rows.shape[1])
        )


def pack_kernel(
    w1_ref, w2_ref, w3_ref, w4_ref, dense_ref, b1_ref, b2_ref, b3_ref, pack_ref, bottom_ref
):
    tail = w1_ref[HEAD_ROWS:, :]
    pack_ref[0, 0:HEAD_ROWS, :] = w1_ref[0:HEAD_ROWS, :]
    pack_ref[1, 0:HEAD_ROWS, :] = jnp.concatenate(
        [tail, jnp.zeros((HEAD_ROWS - tail.shape[0], tail.shape[1]), BF)], axis=0
    )
    for h in range(2):
        at = HEAD_ROWS
        half = w2_ref.shape[0] // 2
        pack_ref[h, at : at + half, :] = w2_ref[h * half : (h + 1) * half, :]
        at += half
        half = w3_ref.shape[0] // 2
        quarter = half // 2
        for q in range(2):
            first = h * half + q * quarter
            pack_ref[h, at : at + quarter, q * 128 : (q + 1) * 128] = w3_ref[first : first + quarter, :]
        at += quarter
        half = w4_ref.shape[1] // 2
        pack_ref[h, at : at + w4_ref.shape[0], :] = w4_ref[:, h * half : (h + 1) * half]
    lower = relu(mm(dense_ref[...], b1_ref[...])).astype(BF)
    middle = relu(mm(lower, b2_ref[...])).astype(BF)
    bottom_ref[...] = relu(mm(middle, b3_ref[...]))


def pick_kernel(meta_ref, side_ref, half_ref):
    half_ref[...] = side_ref[meta_ref[2]]


def lookup_kernel(meta_ref, idx_ref, own_ref, other_ref, out_ref, code_ref, lo_ref, count_ref):
    peers, width = idx_ref.shape
    bags = width // HOT
    span = own_ref.shape[0]
    held = 2 * span
    his = held // LO
    rows = count_ref.shape[0]
    per_chunk = rows // bags
    z, core = meta_ref[1], meta_ref[2]
    rel = idx_ref[...] - z * held
    valid = (rel >= 0) & (rel < held)
    rel = rel ^ (core * span)
    bag = lax.broadcasted_iota(jnp.int32, (peers, width), 1) % bags
    code_ref[...] = jnp.where(valid, (rel // LO) * bags + bag, -1)
    lo_ref[...] = rel % LO
    one, zero = jnp.ones((), BF), jnp.zeros((), BF)

    def one_hot(height, ref, peer):
        ids = lax.broadcasted_iota(jnp.int16, (height, width), 0)
        return jnp.where(ids == ref[pl.ds(peer, 1), :].astype(jnp.int16), one, zero).astype(F8)

    @pl.loop(0, peers // per_chunk)
    def _(chunk):
        for g in range(per_chunk):
            peer = chunk * per_chunk + g
            left = one_hot(his * bags, code_ref, peer)
            counts = mm_t(left, one_hot(LO, lo_ref, peer)).astype(BF)
            for hi in range(his):
                count_ref[g * bags : (g + 1) * bags, hi * LO : (hi + 1) * LO] = counts[
                    hi * bags : (hi + 1) * bags
                ]
        total = mm(count_ref[:, :span], own_ref[...]) + mm(count_ref[:, span:], other_ref[...])
        out_ref[pl.ds(pl.multiple_of(chunk * rows, rows), rows), :] = total


def top_kernel(
    meta_ref, bags_ref, bottom_ref, last_ref, own_ref, side_ref, mirror_ref, near_ref, far_ref,
    out_ref, in_ref, a1_ref, a2_ref, a3_ref,
):
    core, x = meta_ref[2], meta_ref[3]
    reps = last_ref.shape[0]
    peers = bags_ref.shape[0] // TAB
    bottom = bottom_ref[...]
    vectors = [bottom]
    for t in range(TAB):
        total = bags_ref[t * peers]
        for k in range(1, peers):
            total = total + bags_ref[t * peers + k]
        vectors.append(total)
    lane = lax.broadcasted_iota(jnp.int32, bottom.shape, 1)
    pairs = jnp.zeros(bottom.shape, F32)
    at = 0
    for i in range(TAB + 1):
        for j in range(i + 1, TAB + 1):
            dots = jnp.sum(vectors[i] * vectors[j], axis=1, keepdims=True)
            pairs = jnp.where(lane == at, dots, pairs)
            at += 1
    in_ref[0] = bottom.astype(BF)
    in_ref[1] = pairs.astype(BF)

    def whole(ref):
        return [(h, ref.at[h]) for h in range(2)]

    before, after = lax.rem(x + reps - 1, reps), lax.rem(x + 1, reps)
    shards = (
        (x, whole(own_ref)),
        (jnp.where(core == 0, before, after), whole(side_ref)),
        (jnp.where(core == 0, after, before), whole(mirror_ref)),
        (lax.rem(x + 2, reps), [(core, near_ref), (1 - core, far_ref)]),
    )
    for owner, halves in shards:
        y = sum(mm(in_ref[h], w[0:HEAD_ROWS, :]) for h, w in halves)
        a1_ref[owner] = relu(y).astype(BF)
    base = HEAD_ROWS
    for owner, halves in shards:
        y = sum(
            mm(a1_ref[2 * h + q], w[base + q * 256 : base + (q + 1) * 256, :])
            for h, w in halves
            for q in range(2)
        )
        a2_ref[owner] = relu(y).astype(BF)
    base += 512
    for owner, halves in shards:
        y = sum(
            mm(a2_ref[2 * h + q], w[base : base + 256, q * 128 : (q + 1) * 128])
            for h, w in halves
            for q in range(2)
        )
        a3_ref[owner] = relu(y).astype(BF)
    base += 256
    logit = jnp.zeros(out_ref.shape, F32)
    for owner, halves in shards:
        y = sum(
            mm_t(a3_ref[2 * h + q], w[base : base + 64, q * 128 : (q + 1) * 128])
            for h, w in halves
            for q in range(2)
        )
        logit = logit + mm_t(last_ref[owner], relu(y).astype(BF))
    out_ref[...] = logit


def shifted(a, axis, k):
    n = lax.axis_size(axis)
    return lax.ppermute(a, axis, [(i, (i + k) % n) for i in range(n)])


def hold_kernel(in_ref, out_ref):
    pass


def held(a, micros, space):
    spec = pl.BlockSpec(memory_space=space)
    return pl.pallas_call(
        hold_kernel,
        out_shape=jax.ShapeDtypeStruct(a.shape, a.dtype),
        in_specs=[spec],
        out_specs=spec,
        input_output_aliases={0: 0},
        compiler_params=params(4),
        cost_estimate=cost(micros),
        name="held",
    )(a)


def body(tables, indices, bag_lengths, dense, b1, b2, b3, w1, w2, w3, w4, last):
    samples, width = indices.shape[0], tables.shape[1]
    reps = lax.axis_size(X)
    along_z = lax.axis_size(Z)
    peers = lax.axis_size((Y, Z))
    meta = jnp.stack([lax.axis_index(a) for a in ALL]).astype(jnp.int32)
    rows = pl.pallas_call(
        functools.partial(prepare_kernel, along_z),
        out_shape=jax.ShapeDtypeStruct((peers, HOT * samples), jnp.int32),
        in_specs=[pl.BlockSpec(memory_space=pltpu.HBM)] * 2,
        out_specs=VM,
        scratch_shapes=[
            pltpu.VMEM((TAB, HOT, samples), jnp.int32),
            pltpu.VMEM((TAB, samples), jnp.int32),
            pltpu.SemaphoreType.DMA((2,)),
        ],
        compiler_params=params(60),
        cost_estimate=cost(1),
        name="prepare",
    )(jnp.transpose(indices, (1, 2, 0)), jnp.transpose(bag_lengths))
    rows, tables, meta = lax.optimization_barrier((rows, tables, meta))
    wanted = lax.all_to_all(rows, (Y, Z), 0, 0, tiled=True)
    wanted = held(wanted, 60, pltpu.VMEM)
    w4t = jnp.transpose(w4)
    pack_rows = HEAD_ROWS + w2.shape[0] // 2 + w3.shape[0] // 4 + w4t.shape[0]
    pack, bottom = pl.pallas_call(
        pack_kernel,
        out_shape=(
            jax.ShapeDtypeStruct((2, pack_rows, w2.shape[1]), BF),
            jax.ShapeDtypeStruct((samples, width), F32),
        ),
        in_specs=[VM] * 8,
        out_specs=(VM, VM),
        compiler_params=params(8),
        cost_estimate=cost(3),
        name="pack",
    )(w1, w2, w3, w4t, dense, b1, b2, b3)
    sides = [(i, (i + 1) % reps) for i in range(reps)]
    sides += [(reps + i, reps + (i - 1) % reps) for i in range(reps)]
    tables, pack = lax.optimization_barrier((tables, pack))
    other = shifted(tables, C, 1)
    side = lax.ppermute(pack, (C, X), sides)
    partial_bags = pl.pallas_call(
        lookup_kernel,
        out_shape=jax.ShapeDtypeStruct((peers * samples, width), F32),
        in_specs=[SM] + [VM] * 3,
        out_specs=VM,
        scratch_shapes=[
            pltpu.VMEM(wanted.shape, jnp.int32),
            pltpu.VMEM(wanted.shape, jnp.int32),
            pltpu.VMEM((512, 2 * tables.shape[0]), BF),
        ],
        compiler_params=params(14),
        cost_estimate=cost(40),
        name="lookup",
    )(meta, wanted, tables, other)
    side = held(side, 60, pltpu.VMEM)
    mirror = shifted(side, C, 1)
    half = pl.pallas_call(
        pick_kernel,
        out_shape=jax.ShapeDtypeStruct((pack_rows, w2.shape[1]), BF),
        in_specs=[SM, VM],
        out_specs=VM,
        compiler_params=params(4),
        cost_estimate=cost(1),
        name="pick",
    )(meta, side)
    near = lax.ppermute(half, (C, X), sides)
    far = shifted(near, C, 1)
    bags = lax.all_to_all(
        partial_bags.reshape(peers, samples, width), (Y, Z), 0, 0, tiled=True
    )
    logit = pl.pallas_call(
        top_kernel,
        out_shape=jax.ShapeDtypeStruct((1, samples), F32),
        in_specs=[SM] + [VM] * 8,
        out_specs=VM,
        scratch_shapes=[
            pltpu.VMEM((2, samples, width), BF),
            pltpu.VMEM((reps, samples, w1.shape[1]), BF),
            pltpu.VMEM((reps, samples, w2.shape[1]), BF),
            pltpu.VMEM((reps, samples, w3.shape[1]), BF),
        ],
        compiler_params=params(10),
        cost_estimate=cost(5),
        name="top",
    )(meta, bags, bottom, last.reshape(reps, 1, -1), pack, side, mirror, near, far)
    return logit.reshape(samples)


def solution(mesh):
    torus = Mesh(mesh.devices.reshape(8, 8, 2, mesh.shape["rep"]), ALL)
    in_specs = (
        P((Y, Z, C), None),
        P(ALL, None, None),
        P(ALL, None),
        P(ALL, None),
        P(),
        P(),
        P(),
        P(None, X),
        P(None, X),
        P(None, X),
        P(None, X),
        P(),
    )
    return jax.shard_map(body, mesh=torus, in_specs=in_specs, out_specs=P(ALL), check_vma=False)
```

```python
import functools

import jax
import jax.numpy as jnp
from jax import lax
from jax.experimental import pallas as pl
from jax.experimental.pallas import tpu as pltpu
from jax.sharding import Mesh
from jax.sharding import PartitionSpec as P

TAB = 8
HOT = 8
Y, Z, C, X = "y", "z", "c", "x"
ALL = (Y, Z, C, X)
LO = 256
HEAD_ROWS = 128
BF = jnp.bfloat16
F8 = jnp.float8_e4m3fn
F32 = jnp.float32
VM = pl.BlockSpec(memory_space=pltpu.VMEM)
SM = pl.BlockSpec(memory_space=pltpu.SMEM)
LANES = (((1,), (1,)), ((), ()))


def mm(a, b):
    return jnp.dot(a, b, preferred_element_type=F32)


def mm_t(a, b):
    return lax.dot_general(a, b, LANES, preferred_element_type=F32)


def relu(a):
    return jnp.maximum(a, 0.0)


def cost(micros):
    return pl.CostEstimate(flops=int(micros * 1.0e9), bytes_accessed=1 << 20, transcendentals=0)


def params(mib):
    return pltpu.CompilerParams(vmem_limit_bytes=mib << 20)


def prepare_kernel(peers, idx_hbm, len_hbm, out_ref, idx_ref, len_ref, sem):
    copies = [
        pltpu.make_async_copy(idx_hbm, idx_ref, sem.at[0]),
        pltpu.make_async_copy(len_hbm, len_ref, sem.at[1]),
    ]
    for copy in copies:
        copy.start()
    for copy in copies:
        copy.wait()
    lens = len_ref[...]
    parts = [jnp.where(lens > h, idx_ref[:, h, :], -1) for h in range(HOT)]
    rows = jnp.concatenate(parts, axis=1)
    for t in range(TAB):
        out_ref[t * peers : (t + 1) * peers, :] = jnp.broadcast_to(
            rows[t : t + 1, :], (peers, rows.shape[1])
        )


def pack_kernel(
    w1_ref, w2_ref, w3_ref, w4_ref, dense_ref, b1_ref, b2_ref, b3_ref, pack_ref, bottom_ref
):
    tail = w1_ref[HEAD_ROWS:, :]
    pack_ref[0, 0:HEAD_ROWS, :] = w1_ref[0:HEAD_ROWS, :]
    pack_ref[1, 0:HEAD_ROWS, :] = jnp.concatenate(
        [tail, jnp.zeros((HEAD_ROWS - tail.shape[0], tail.shape[1]), BF)], axis=0
    )
    for h in range(2):
        at = HEAD_ROWS
        half = w2_ref.shape[0] // 2
        pack_ref[h, at : at + half, :] = w2_ref[h * half : (h + 1) * half, :]
        at += half
        half = w3_ref.shape[0] // 2
        quarter = half // 2
        for q in range(2):
            first = h * half + q * quarter
            pack_ref[h, at : at + quarter, q * 128 : (q + 1) * 128] = w3_ref[first : first + quarter, :]
        at += quarter
        half = w4_ref.shape[1] // 2
        pack_ref[h, at : at + w4_ref.shape[0], :] = w4_ref[:, h * half : (h + 1) * half]
    lower = relu(mm(dense_ref[...], b1_ref[...])).astype(BF)
    middle = relu(mm(lower, b2_ref[...])).astype(BF)
    bottom_ref[...] = relu(mm(middle, b3_ref[...]))


def lookup_kernel(meta_ref, idx_ref, own_ref, other_ref, out_ref, code_ref, lo_ref, count_ref):
    peers, width = idx_ref.shape
    bags = width // HOT
    span = own_ref.shape[0]
    held = 2 * span
    his = held // LO
    rows = count_ref.shape[0]
    per_chunk = rows // bags
    z, core = meta_ref[1], meta_ref[2]
    rel = idx_ref[...] - z * held
    valid = (rel >= 0) & (rel < held)
    rel = rel ^ (core * span)
    bag = lax.broadcasted_iota(jnp.int32, (peers, width), 1) % bags
    code_ref[...] = jnp.where(valid, (rel // LO) * bags + bag, -1)
    lo_ref[...] = rel % LO
    one, zero = jnp.ones((), BF), jnp.zeros((), BF)

    def one_hot(height, ref, peer):
        ids = lax.broadcasted_iota(jnp.int16, (height, width), 0)
        return jnp.where(ids == ref[pl.ds(peer, 1), :].astype(jnp.int16), one, zero).astype(F8)

    @pl.loop(0, peers // per_chunk)
    def _(chunk):
        for g in range(per_chunk):
            peer = chunk * per_chunk + g
            left = one_hot(his * bags, code_ref, peer)
            counts = mm_t(left, one_hot(LO, lo_ref, peer)).astype(BF)
            for hi in range(his):
                count_ref[g * bags : (g + 1) * bags, hi * LO : (hi + 1) * LO] = counts[
                    hi * bags : (hi + 1) * bags
                ]
        total = mm(count_ref[:, :span], own_ref[...]) + mm(count_ref[:, span:], other_ref[...])
        out_ref[pl.ds(pl.multiple_of(chunk * rows, rows), rows), :] = total


def top_kernel(
    meta_ref, bags_ref, bottom_ref, last_ref, own_ref, side_ref, mirror_ref, across_ref,
    out_ref, in_ref, a1_ref, a2_ref, a3_ref,
):
    core, x = meta_ref[2], meta_ref[3]
    reps = last_ref.shape[0]
    peers = bags_ref.shape[0] // TAB
    bottom = bottom_ref[...]
    vectors = [bottom]
    for t in range(TAB):
        total = bags_ref[t * peers]
        for k in range(1, peers):
            total = total + bags_ref[t * peers + k]
        vectors.append(total)
    lane = lax.broadcasted_iota(jnp.int32, bottom.shape, 1)
    pairs = jnp.zeros(bottom.shape, F32)
    at = 0
    for i in range(TAB + 1):
        for j in range(i + 1, TAB + 1):
            dots = jnp.sum(vectors[i] * vectors[j], axis=1, keepdims=True)
            pairs = jnp.where(lane == at, dots, pairs)
            at += 1
    in_ref[0] = bottom.astype(BF)
    in_ref[1] = pairs.astype(BF)

    def whole(ref):
        return [(h, ref.at[h]) for h in range(2)]

    before, after = lax.rem(x + reps - 1, reps), lax.rem(x + 1, reps)
    shards = (
        (x, whole(own_ref)),
        (jnp.where(core == 0, before, after), whole(side_ref)),
        (jnp.where(core == 0, after, before), whole(mirror_ref)),
        (lax.rem(x + 2, reps), whole(across_ref)),
    )
    for owner, halves in shards:
        y = sum(mm(in_ref[h], w[0:HEAD_ROWS, :]) for h, w in halves)
        a1_ref[owner] = relu(y).astype(BF)
    base = HEAD_ROWS
    for owner, halves in shards:
        y = sum(
            mm(a1_ref[2 * h + q], w[base + q * 256 : base + (q + 1) * 256, :])
            for h, w in halves
            for q in range(2)
        )
        a2_ref[owner] = relu(y).astype(BF)
    base += 512
    for owner, halves in shards:
        y = sum(
            mm(a2_ref[2 * h + q], w[base : base + 256, q * 128 : (q + 1) * 128])
            for h, w in halves
            for q in range(2)
        )
        a3_ref[owner] = relu(y).astype(BF)
    base += 256
    logit = jnp.zeros(out_ref.shape, F32)
    for owner, halves in shards:
        y = sum(
            mm_t(a3_ref[2 * h + q], w[base : base + 64, q * 128 : (q + 1) * 128])
            for h, w in halves
            for q in range(2)
        )
        logit = logit + mm_t(last_ref[owner], relu(y).astype(BF))
    out_ref[...] = logit


def shifted(a, axis, k):
    n = lax.axis_size(axis)
    return lax.ppermute(a, axis, [(i, (i + k) % n) for i in range(n)])


def hold_kernel(in_ref, out_ref):
    pass


def held(a, micros, space):
    spec = pl.BlockSpec(memory_space=space)
    return pl.pallas_call(
        hold_kernel,
        out_shape=jax.ShapeDtypeStruct(a.shape, a.dtype),
        in_specs=[spec],
        out_specs=spec,
        input_output_aliases={0: 0},
        compiler_params=params(4),
        cost_estimate=cost(micros),
        name="held",
    )(a)


def body(tables, indices, bag_lengths, dense, b1, b2, b3, w1, w2, w3, w4, last):
    samples, width = indices.shape[0], tables.shape[1]
    reps = lax.axis_size(X)
    along_z = lax.axis_size(Z)
    peers = lax.axis_size((Y, Z))
    meta = jnp.stack([lax.axis_index(a) for a in ALL]).astype(jnp.int32)
    rows = pl.pallas_call(
        functools.partial(prepare_kernel, along_z),
        out_shape=jax.ShapeDtypeStruct((peers, HOT * samples), jnp.int32),
        in_specs=[pl.BlockSpec(memory_space=pltpu.HBM)] * 2,
        out_specs=VM,
        scratch_shapes=[
            pltpu.VMEM((TAB, HOT, samples), jnp.int32),
            pltpu.VMEM((TAB, samples), jnp.int32),
            pltpu.SemaphoreType.DMA((2,)),
        ],
        compiler_params=params(60),
        cost_estimate=cost(1),
        name="prepare",
    )(jnp.transpose(indices, (1, 2, 0)), jnp.transpose(bag_lengths))
    rows, tables, meta = lax.optimization_barrier((rows, tables, meta))
    wanted = lax.all_to_all(rows, (Y, Z), 0, 0, tiled=True)
    wanted = held(wanted, 60, pltpu.VMEM)
    w4t = jnp.transpose(w4)
    pack_rows = HEAD_ROWS + w2.shape[0] // 2 + w3.shape[0] // 4 + w4t.shape[0]
    pack, bottom = pl.pallas_call(
        pack_kernel,
        out_shape=(
            jax.ShapeDtypeStruct((2, pack_rows, w2.shape[1]), BF),
            jax.ShapeDtypeStruct((samples, width), F32),
        ),
        in_specs=[VM] * 8,
        out_specs=(VM, VM),
        compiler_params=params(8),
        cost_estimate=cost(3),
        name="pack",
    )(w1, w2, w3, w4t, dense, b1, b2, b3)
    sides = [(i, (i + 1) % reps) for i in range(reps)]
    sides += [(reps + i, reps + (i - 1) % reps) for i in range(reps)]
    tables, pack = lax.optimization_barrier((tables, pack))
    other = shifted(tables, C, 1)
    side = lax.ppermute(pack, (C, X), sides)
    partial_bags = pl.pallas_call(
        lookup_kernel,
        out_shape=jax.ShapeDtypeStruct((peers * samples, width), F32),
        in_specs=[SM] + [VM] * 3,
        out_specs=VM,
        scratch_shapes=[
            pltpu.VMEM(wanted.shape, jnp.int32),
            pltpu.VMEM(wanted.shape, jnp.int32),
            pltpu.VMEM((512, 2 * tables.shape[0]), BF),
        ],
        compiler_params=params(14),
        cost_estimate=cost(40),
        name="lookup",
    )(meta, wanted, tables, other)
    side = held(side, 60, pltpu.VMEM)
    mirror = shifted(side, C, 1)
    across = lax.ppermute(side, (C, X), sides)
    bags = lax.all_to_all(
        partial_bags.reshape(peers, samples, width), (Y, Z), 0, 0, tiled=True
    )
    logit = pl.pallas_call(
        top_kernel,
        out_shape=jax.ShapeDtypeStruct((1, samples), F32),
        in_specs=[SM] + [VM] * 7,
        out_specs=VM,
        scratch_shapes=[
            pltpu.VMEM((2, samples, width), BF),
            pltpu.VMEM((reps, samples, w1.shape[1]), BF),
            pltpu.VMEM((reps, samples, w2.shape[1]), BF),
            pltpu.VMEM((reps, samples, w3.shape[1]), BF),
        ],
        compiler_params=params(10),
        cost_estimate=cost(5),
        name="top",
    )(meta, bags, bottom, last.reshape(reps, 1, -1), pack, side, mirror, across)
    return logit.reshape(samples)


def solution(mesh):
    torus = Mesh(mesh.devices.reshape(8, 8, 2, mesh.shape["rep"]), ALL)
    in_specs = (
        P((Y, Z, C), None),
        P(ALL, None, None),
        P(ALL, None),
        P(ALL, None),
        P(),
        P(),
        P(),
        P(None, X),
        P(None, X),
        P(None, X),
        P(None, X),
        P(),
    )
    return jax.shard_map(body, mesh=torus, in_specs=in_specs, out_specs=P(ALL), check_vma=False)
```

```python
import functools

import jax
import jax.numpy as jnp
from jax import lax
from jax.experimental import pallas as pl
from jax.experimental.pallas import tpu as pltpu
from jax.sharding import Mesh
from jax.sharding import PartitionSpec as P

TAB = 8
HOT = 8
Y, Z, N, C, X = "y", "z", "n", "c", "x"
ALL = (Y, Z, N, C, X)
LO = 256
HEAD_ROWS = 128
BF = jnp.bfloat16
F8 = jnp.float8_e4m3fn
F32 = jnp.float32
VM = pl.BlockSpec(memory_space=pltpu.VMEM)
SM = pl.BlockSpec(memory_space=pltpu.SMEM)
LANES = (((1,), (1,)), ((), ()))


def mm(a, b):
    return jnp.dot(a, b, preferred_element_type=F32)


def mm_t(a, b):
    return lax.dot_general(a, b, LANES, preferred_element_type=F32)


def relu(a):
    return jnp.maximum(a, 0.0)


def cost(micros):
    return pl.CostEstimate(flops=int(micros * 1.0e9), bytes_accessed=1 << 20, transcendentals=0)


def params(mib):
    return pltpu.CompilerParams(vmem_limit_bytes=mib << 20)


def prepare_kernel(peers, idx_hbm, len_hbm, out_ref, idx_ref, len_ref, sem):
    copies = [
        pltpu.make_async_copy(idx_hbm, idx_ref, sem.at[0]),
        pltpu.make_async_copy(len_hbm, len_ref, sem.at[1]),
    ]
    for copy in copies:
        copy.start()
    for copy in copies:
        copy.wait()
    lens = len_ref[...]
    parts = [jnp.where(lens > h, idx_ref[:, h, :], -1) for h in range(HOT)]
    rows = jnp.concatenate(parts, axis=1)
    for t in range(TAB):
        out_ref[t * peers : (t + 1) * peers, :] = jnp.broadcast_to(
            rows[t : t + 1, :], (peers, rows.shape[1])
        )


def pack_kernel(
    w1_ref, w2_ref, w3_ref, w4_ref, dense_ref, b1_ref, b2_ref, b3_ref, pack_ref, bottom_ref
):
    tail = w1_ref[HEAD_ROWS:, :]
    pack_ref[0, 0:HEAD_ROWS, :] = w1_ref[0:HEAD_ROWS, :]
    pack_ref[1, 0:HEAD_ROWS, :] = jnp.concatenate(
        [tail, jnp.zeros((HEAD_ROWS - tail.shape[0], tail.shape[1]), BF)], axis=0
    )
    for h in range(2):
        at = HEAD_ROWS
        half = w2_ref.shape[0] // 2
        pack_ref[h, at : at + half, :] = w2_ref[h * half : (h + 1) * half, :]
        at += half
        half = w3_ref.shape[0] // 2
        quarter = half // 2
        for q in range(2):
            first = h * half + q * quarter
            pack_ref[h, at : at + quarter, q * 128 : (q + 1) * 128] = w3_ref[first : first + quarter, :]
        at += quarter
        half = w4_ref.shape[1] // 2
        pack_ref[h, at : at + w4_ref.shape[0], :] = w4_ref[:, h * half : (h + 1) * half]
    lower = relu(mm(dense_ref[...], b1_ref[...])).astype(BF)
    middle = relu(mm(lower, b2_ref[...])).astype(BF)
    bottom_ref[...] = relu(mm(middle, b3_ref[...]))


def lookup_kernel(meta_ref, idx_ref, same_ref, other_ref, out_ref, code_ref, lo_ref, count_ref):
    peers, width = idx_ref.shape
    bags = width // HOT
    near, span = same_ref.shape[0], same_ref.shape[1]
    held = 2 * near * span
    his = held // LO
    rows = count_ref.shape[0]
    per_chunk = rows // bags
    z, n, core = meta_ref[1], meta_ref[2], meta_ref[3]
    rel = idx_ref[...] - z * held
    valid = (rel >= 0) & (rel < held)
    rel = rel ^ ((n * 2 + core) * span)
    bag = lax.broadcasted_iota(jnp.int32, (peers, width), 1) % bags
    code_ref[...] = jnp.where(valid, (rel // LO) * bags + bag, -1)
    lo_ref[...] = rel % LO
    one, zero = jnp.ones((), BF), jnp.zeros((), BF)

    def one_hot(height, ref, peer):
        ids = lax.broadcasted_iota(jnp.int16, (height, width), 0)
        return jnp.where(ids == ref[pl.ds(peer, 1), :].astype(jnp.int16), one, zero).astype(F8)

    @pl.loop(0, peers // per_chunk)
    def _(chunk):
        for g in range(per_chunk):
            peer = chunk * per_chunk + g
            left = one_hot(his * bags, code_ref, peer)
            counts = mm_t(left, one_hot(LO, lo_ref, peer)).astype(BF)
            for hi in range(his):
                count_ref[g * bags : (g + 1) * bags, hi * LO : (hi + 1) * LO] = counts[
                    hi * bags : (hi + 1) * bags
                ]
        blocks = [ref[k] for k in range(near) for ref in (same_ref, other_ref)]
        total = sum(mm(count_ref[:, k * span : (k + 1) * span], b) for k, b in enumerate(blocks))
        out_ref[pl.ds(pl.multiple_of(chunk * rows, rows), rows), :] = total


def top_kernel(
    meta_ref, bags_ref, bottom_ref, last_ref, own_ref, side_ref, across_ref, mirror_ref,
    out_ref, in_ref, a1_ref, a2_ref, a3_ref,
):
    core, x = meta_ref[3], meta_ref[4]
    reps = last_ref.shape[0]
    peers = bags_ref.shape[0] // TAB
    bottom = bottom_ref[...]
    vectors = [bottom]
    for t in range(TAB):
        total = bags_ref[t * peers]
        for k in range(1, peers):
            total = total + bags_ref[t * peers + k]
        vectors.append(total)
    lane = lax.broadcasted_iota(jnp.int32, bottom.shape, 1)
    pairs = jnp.zeros(bottom.shape, F32)
    at = 0
    for i in range(TAB + 1):
        for j in range(i + 1, TAB + 1):
            dots = jnp.sum(vectors[i] * vectors[j], axis=1, keepdims=True)
            pairs = jnp.where(lane == at, dots, pairs)
            at += 1
    in_ref[0] = bottom.astype(BF)
    in_ref[1] = pairs.astype(BF)

    def whole(ref):
        return [(h, ref.at[h]) for h in range(2)]

    before, after = lax.rem(x + reps - 1, reps), lax.rem(x + 1, reps)
    shards = (
        (x, whole(own_ref)),
        (jnp.where(core == 0, before, after), whole(side_ref)),
        (jnp.where(core == 0, after, before), whole(mirror_ref)),
        (lax.rem(x + 2, reps), whole(across_ref)),
    )
    for owner, halves in shards:
        y = sum(mm(in_ref[h], w[0:HEAD_ROWS, :]) for h, w in halves)
        a1_ref[owner] = relu(y).astype(BF)
    base = HEAD_ROWS
    for owner, halves in shards:
        y = sum(
            mm(a1_ref[2 * h + q], w[base + q * 256 : base + (q + 1) * 256, :])
            for h, w in halves
            for q in range(2)
        )
        a2_ref[owner] = relu(y).astype(BF)
    base += 512
    for owner, halves in shards:
        y = sum(
            mm(a2_ref[2 * h + q], w[base : base + 256, q * 128 : (q + 1) * 128])
            for h, w in halves
            for q in range(2)
        )
        a3_ref[owner] = relu(y).astype(BF)
    base += 256
    logit = jnp.zeros(out_ref.shape, F32)
    for owner, halves in shards:
        y = sum(
            mm_t(a3_ref[2 * h + q], w[base : base + 64, q * 128 : (q + 1) * 128])
            for h, w in halves
            for q in range(2)
        )
        logit = logit + mm_t(last_ref[owner], relu(y).astype(BF))
    out_ref[...] = logit


def shifted(a, axis, k):
    n = lax.axis_size(axis)
    return lax.ppermute(a, axis, [(i, (i + k) % n) for i in range(n)])


def hold_kernel(in_ref, out_ref):
    pass


def held(a, micros, space):
    spec = pl.BlockSpec(memory_space=space)
    return pl.pallas_call(
        hold_kernel,
        out_shape=jax.ShapeDtypeStruct(a.shape, a.dtype),
        in_specs=[spec],
        out_specs=spec,
        input_output_aliases={0: 0},
        compiler_params=params(4),
        cost_estimate=cost(micros),
        name="held",
    )(a)


def body(tables, indices, bag_lengths, dense, b1, b2, b3, w1, w2, w3, w4, last):
    samples, width = indices.shape[0], tables.shape[1]
    reps = lax.axis_size(X)
    along_z = lax.axis_size(Z)
    pair = lax.axis_size(N)
    peers = lax.axis_size((Y, Z))
    meta = jnp.stack([lax.axis_index(a) for a in ALL]).astype(jnp.int32)
    rows = pl.pallas_call(
        functools.partial(prepare_kernel, along_z),
        out_shape=jax.ShapeDtypeStruct((peers, HOT * samples), jnp.int32),
        in_specs=[pl.BlockSpec(memory_space=pltpu.HBM)] * 2,
        out_specs=VM,
        scratch_shapes=[
            pltpu.VMEM((TAB, HOT, samples), jnp.int32),
            pltpu.VMEM((TAB, samples), jnp.int32),
            pltpu.SemaphoreType.DMA((2,)),
        ],
        compiler_params=params(60),
        cost_estimate=cost(1),
        name="prepare",
    )(jnp.transpose(indices, (1, 2, 0)), jnp.transpose(bag_lengths))
    rows, tables, meta = lax.optimization_barrier((rows, tables, meta))
    wanted = lax.all_to_all(rows, (Y, Z), 0, 0, tiled=True)
    wanted = held(wanted, 60, pltpu.VMEM)
    beside = shifted(tables, N, 1)
    w4t = jnp.transpose(w4)
    pack_rows = HEAD_ROWS + w2.shape[0] // 2 + w3.shape[0] // 4 + w4t.shape[0]
    pack, bottom = pl.pallas_call(
        pack_kernel,
        out_shape=(
            jax.ShapeDtypeStruct((2, pack_rows, w2.shape[1]), BF),
            jax.ShapeDtypeStruct((samples, width), F32),
        ),
        in_specs=[VM] * 8,
        out_specs=(VM, VM),
        compiler_params=params(8),
        cost_estimate=cost(3),
        name="pack",
    )(w1, w2, w3, w4t, dense, b1, b2, b3)
    sides = [(i, (i + 1) % reps) for i in range(reps)]
    sides += [(reps + i, reps + (i - 1) % reps) for i in range(reps)]
    beside, pack = lax.optimization_barrier((beside, pack))
    same = jnp.stack([tables, beside])
    other = shifted(same, C, 1)
    side = lax.ppermute(pack, (C, X), sides)
    partial_bags = pl.pallas_call(
        lookup_kernel,
        out_shape=jax.ShapeDtypeStruct((peers * samples, width), F32),
        in_specs=[SM] + [VM] * 3,
        out_specs=VM,
        scratch_shapes=[
            pltpu.VMEM(wanted.shape, jnp.int32),
            pltpu.VMEM(wanted.shape, jnp.int32),
            pltpu.VMEM((256, 2 * pair * tables.shape[0]), BF),
        ],
        compiler_params=params(14),
        cost_estimate=cost(1),
        name="lookup",
    )(meta, wanted, same, other)
    side = held(side, 60, pl.ANY)
    across = lax.ppermute(side, (C, X), sides)
    mirror = shifted(side, C, 1)
    bags = lax.all_to_all(
        partial_bags.reshape(peers, samples, width), (Y, Z), 0, 0, tiled=True
    )
    bags = held(bags, 300, pltpu.VMEM)
    logit = pl.pallas_call(
        top_kernel,
        out_shape=jax.ShapeDtypeStruct((1, samples), F32),
        in_specs=[SM] + [VM] * 7,
        out_specs=VM,
        scratch_shapes=[
            pltpu.VMEM((2, samples, width), BF),
            pltpu.VMEM((reps, samples, w1.shape[1]), BF),
            pltpu.VMEM((reps, samples, w2.shape[1]), BF),
            pltpu.VMEM((reps, samples, w3.shape[1]), BF),
        ],
        compiler_params=params(10),
        cost_estimate=cost(5),
        name="top",
    )(meta, bags, bottom, last.reshape(reps, 1, -1), pack, side, across, mirror)
    return logit.reshape(samples)


def solution(mesh):
    torus = Mesh(mesh.devices.reshape(8, 4, 2, 2, mesh.shape["rep"]), ALL)
    in_specs = (
        P((Y, Z, N, C), None),
        P(ALL, None, None),
        P(ALL, None),
        P(ALL, None),
        P(),
        P(),
        P(),
        P(None, X),
        P(None, X),
        P(None, X),
        P(None, X),
        P(),
    )
    return jax.shard_map(body, mesh=torus, in_specs=in_specs, out_specs=P(ALL), check_vma=False)
```

```python
import functools

import jax
import jax.numpy as jnp
from jax import lax
from jax.experimental import pallas as pl
from jax.experimental.pallas import tpu as pltpu
from jax.sharding import Mesh
from jax.sharding import PartitionSpec as P

TAB = 8
HOT = 8
Y, Z, C, X = "y", "z", "c", "x"
ALL = (Y, Z, C, X)
LO = 256
HEAD_ROWS = 128
BF = jnp.bfloat16
F8 = jnp.float8_e4m3fn
F32 = jnp.float32
VM = pl.BlockSpec(memory_space=pltpu.VMEM)
SM = pl.BlockSpec(memory_space=pltpu.SMEM)
LANES = (((1,), (1,)), ((), ()))


def mm(a, b):
    return jnp.dot(a, b, preferred_element_type=F32)


def mm_t(a, b):
    return lax.dot_general(a, b, LANES, preferred_element_type=F32)


def relu(a):
    return jnp.maximum(a, 0.0)


def cost(micros):
    return pl.CostEstimate(flops=int(micros * 1.0e9), bytes_accessed=1 << 20, transcendentals=0)


def params(mib):
    return pltpu.CompilerParams(vmem_limit_bytes=mib << 20)


def prepare_kernel(peers, idx_hbm, len_hbm, out_ref, idx_ref, len_ref, sem):
    copies = [
        pltpu.make_async_copy(idx_hbm, idx_ref, sem.at[0]),
        pltpu.make_async_copy(len_hbm, len_ref, sem.at[1]),
    ]
    for copy in copies:
        copy.start()
    for copy in copies:
        copy.wait()
    lens = len_ref[...]
    parts = [jnp.where(lens > h, idx_ref[:, h, :], -1) for h in range(HOT)]
    rows = jnp.concatenate(parts, axis=1)
    for t in range(TAB):
        out_ref[t * peers : (t + 1) * peers, :] = jnp.broadcast_to(
            rows[t : t + 1, :], (peers, rows.shape[1])
        )


def pack_kernel(
    w1_ref, w2_ref, w3_ref, w4_ref, dense_ref, b1_ref, b2_ref, b3_ref, pack_ref, bottom_ref
):
    tail = w1_ref[HEAD_ROWS:, :]
    pack_ref[0, 0:HEAD_ROWS, :] = w1_ref[0:HEAD_ROWS, :]
    pack_ref[1, 0:HEAD_ROWS, :] = jnp.concatenate(
        [tail, jnp.zeros((HEAD_ROWS - tail.shape[0], tail.shape[1]), BF)], axis=0
    )
    for h in range(2):
        at = HEAD_ROWS
        half = w2_ref.shape[0] // 2
        pack_ref[h, at : at + half, :] = w2_ref[h * half : (h + 1) * half, :]
        at += half
        half = w3_ref.shape[0] // 2
        quarter = half // 2
        for q in range(2):
            first = h * half + q * quarter
            pack_ref[h, at : at + quarter, q * 128 : (q + 1) * 128] = w3_ref[first : first + quarter, :]
        at += quarter
        half = w4_ref.shape[1] // 2
        pack_ref[h, at : at + w4_ref.shape[0], :] = w4_ref[:, h * half : (h + 1) * half]
    lower = relu(mm(dense_ref[...], b1_ref[...])).astype(BF)
    middle = relu(mm(lower, b2_ref[...])).astype(BF)
    bottom_ref[...] = relu(mm(middle, b3_ref[...]))


def lookup_kernel(meta_ref, idx_ref, own_ref, other_ref, out_ref, code_ref, lo_ref, count_ref):
    peers, width = idx_ref.shape
    bags = width // HOT
    span = own_ref.shape[0]
    held = 2 * span
    his = held // LO
    rows = count_ref.shape[0]
    per_chunk = rows // bags
    z, core = meta_ref[1], meta_ref[2]
    rel = idx_ref[...] - z * held
    valid = (rel >= 0) & (rel < held)
    rel = rel ^ (core * span)
    bag = lax.broadcasted_iota(jnp.int32, (peers, width), 1) % bags
    code_ref[...] = jnp.where(valid, (rel // LO) * bags + bag, -1)
    lo_ref[...] = rel % LO
    one, zero = jnp.ones((), BF), jnp.zeros((), BF)

    def one_hot(height, ref, peer):
        ids = lax.broadcasted_iota(jnp.int16, (height, width), 0)
        return jnp.where(ids == ref[pl.ds(peer, 1), :].astype(jnp.int16), one, zero).astype(F8)

    @pl.loop(0, peers // per_chunk)
    def _(chunk):
        for g in range(per_chunk):
            peer = chunk * per_chunk + g
            left = one_hot(his * bags, code_ref, peer)
            counts = mm_t(left, one_hot(LO, lo_ref, peer)).astype(BF)
            for hi in range(his):
                count_ref[g * bags : (g + 1) * bags, hi * LO : (hi + 1) * LO] = counts[
                    hi * bags : (hi + 1) * bags
                ]
        total = mm(count_ref[:, :span], own_ref[...]) + mm(count_ref[:, span:], other_ref[...])
        out_ref[pl.ds(pl.multiple_of(chunk * rows, rows), rows), :] = total


def top_kernel(
    meta_ref, bags_ref, bottom_ref, last_ref, own_ref, side_ref, across_ref, mirror_ref,
    out_ref, in_ref, a1_ref, a2_ref, a3_ref,
):
    core, x = meta_ref[2], meta_ref[3]
    reps = last_ref.shape[0]
    peers = bags_ref.shape[0] // TAB
    bottom = bottom_ref[...]
    vectors = [bottom]
    for t in range(TAB):
        total = bags_ref[t * peers]
        for k in range(1, peers):
            total = total + bags_ref[t * peers + k]
        vectors.append(total)
    lane = lax.broadcasted_iota(jnp.int32, bottom.shape, 1)
    pairs = jnp.zeros(bottom.shape, F32)
    at = 0
    for i in range(TAB + 1):
        for j in range(i + 1, TAB + 1):
            dots = jnp.sum(vectors[i] * vectors[j], axis=1, keepdims=True)
            pairs = jnp.where(lane == at, dots, pairs)
            at += 1
    in_ref[0] = bottom.astype(BF)
    in_ref[1] = pairs.astype(BF)

    def whole(ref):
        return [(h, ref.at[h]) for h in range(2)]

    before, after = lax.rem(x + reps - 1, reps), lax.rem(x + 1, reps)
    shards = (
        (x, whole(own_ref)),
        (jnp.where(core == 0, before, after), whole(side_ref)),
        (jnp.where(core == 0, after, before), whole(mirror_ref)),
        (lax.rem(x + 2, reps), whole(across_ref)),
    )
    for owner, halves in shards:
        y = sum(mm(in_ref[h], w[0:HEAD_ROWS, :]) for h, w in halves)
        a1_ref[owner] = relu(y).astype(BF)
    base = HEAD_ROWS
    for owner, halves in shards:
        y = sum(
            mm(a1_ref[2 * h + q], w[base + q * 256 : base + (q + 1) * 256, :])
            for h, w in halves
            for q in range(2)
        )
        a2_ref[owner] = relu(y).astype(BF)
    base += 512
    for owner, halves in shards:
        y = sum(
            mm(a2_ref[2 * h + q], w[base : base + 256, q * 128 : (q + 1) * 128])
            for h, w in halves
            for q in range(2)
        )
        a3_ref[owner] = relu(y).astype(BF)
    base += 256
    logit = jnp.zeros(out_ref.shape, F32)
    for owner, halves in shards:
        y = sum(
            mm_t(a3_ref[2 * h + q], w[base : base + 64, q * 128 : (q + 1) * 128])
            for h, w in halves
            for q in range(2)
        )
        logit = logit + mm_t(last_ref[owner], relu(y).astype(BF))
    out_ref[...] = logit


def shifted(a, axis, k):
    n = lax.axis_size(axis)
    return lax.ppermute(a, axis, [(i, (i + k) % n) for i in range(n)])


def hold_kernel(in_ref, out_ref):
    pass


def held(a, micros, space):
    spec = pl.BlockSpec(memory_space=space)
    return pl.pallas_call(
        hold_kernel,
        out_shape=jax.ShapeDtypeStruct(a.shape, a.dtype),
        in_specs=[spec],
        out_specs=spec,
        input_output_aliases={0: 0},
        compiler_params=params(4),
        cost_estimate=cost(micros),
        name="held",
    )(a)


def body(tables, indices, bag_lengths, dense, b1, b2, b3, w1, w2, w3, w4, last):
    samples, width = indices.shape[0], tables.shape[1]
    reps = lax.axis_size(X)
    along_z = lax.axis_size(Z)
    peers = lax.axis_size((Y, Z))
    meta = jnp.stack([lax.axis_index(a) for a in ALL]).astype(jnp.int32)
    rows = pl.pallas_call(
        functools.partial(prepare_kernel, along_z),
        out_shape=jax.ShapeDtypeStruct((peers, HOT * samples), jnp.int32),
        in_specs=[pl.BlockSpec(memory_space=pltpu.HBM)] * 2,
        out_specs=VM,
        scratch_shapes=[
            pltpu.VMEM((TAB, HOT, samples), jnp.int32),
            pltpu.VMEM((TAB, samples), jnp.int32),
            pltpu.SemaphoreType.DMA((2,)),
        ],
        compiler_params=params(60),
        cost_estimate=cost(1),
        name="prepare",
    )(jnp.transpose(indices, (1, 2, 0)), jnp.transpose(bag_lengths))
    rows, tables, meta = lax.optimization_barrier((rows, tables, meta))
    wanted = lax.all_to_all(rows, (Y, Z), 0, 0, tiled=True)
    wanted = held(wanted, 60, pltpu.VMEM)
    w4t = jnp.transpose(w4)
    pack_rows = HEAD_ROWS + w2.shape[0] // 2 + w3.shape[0] // 4 + w4t.shape[0]
    pack, bottom = pl.pallas_call(
        pack_kernel,
        out_shape=(
            jax.ShapeDtypeStruct((2, pack_rows, w2.shape[1]), BF),
            jax.ShapeDtypeStruct((samples, width), F32),
        ),
        in_specs=[VM] * 8,
        out_specs=(VM, VM),
        compiler_params=params(8),
        cost_estimate=cost(3),
        name="pack",
    )(w1, w2, w3, w4t, dense, b1, b2, b3)
    sides = [(i, (i + 1) % reps) for i in range(reps)]
    sides += [(reps + i, reps + (i - 1) % reps) for i in range(reps)]
    tables, pack = lax.optimization_barrier((tables, pack))
    other = shifted(tables, C, 1)
    side = lax.ppermute(pack, (C, X), sides)
    partial_bags = pl.pallas_call(
        lookup_kernel,
        out_shape=jax.ShapeDtypeStruct((peers * samples, width), F32),
        in_specs=[SM] + [VM] * 3,
        out_specs=VM,
        scratch_shapes=[
            pltpu.VMEM(wanted.shape, jnp.int32),
            pltpu.VMEM(wanted.shape, jnp.int32),
            pltpu.VMEM((512, 2 * tables.shape[0]), BF),
        ],
        compiler_params=params(14),
        cost_estimate=cost(40),
        name="lookup",
    )(meta, wanted, tables, other)
    side = held(side, 60, pltpu.VMEM)
    across = lax.ppermute(side, (C, X), sides)
    mirror = shifted(side, C, 1)
    bags = lax.all_to_all(
        partial_bags.reshape(peers, samples, width), (Y, Z), 0, 0, tiled=True
    )
    bags = held(bags, 15, pltpu.VMEM)
    logit = pl.pallas_call(
        top_kernel,
        out_shape=jax.ShapeDtypeStruct((1, samples), F32),
        in_specs=[SM] + [VM] * 7,
        out_specs=VM,
        scratch_shapes=[
            pltpu.VMEM((2, samples, width), BF),
            pltpu.VMEM((reps, samples, w1.shape[1]), BF),
            pltpu.VMEM((reps, samples, w2.shape[1]), BF),
            pltpu.VMEM((reps, samples, w3.shape[1]), BF),
        ],
        compiler_params=params(10),
        cost_estimate=cost(5),
        name="top",
    )(meta, bags, bottom, last.reshape(reps, 1, -1), pack, side, across, mirror)
    return logit.reshape(samples)


def solution(mesh):
    torus = Mesh(mesh.devices.reshape(8, 8, 2, mesh.shape["rep"]), ALL)
    in_specs = (
        P((Y, Z, C), None),
        P(ALL, None, None),
        P(ALL, None),
        P(ALL, None),
        P(),
        P(),
        P(),
        P(None, X),
        P(None, X),
        P(None, X),
        P(None, X),
        P(),
    )
    return jax.shard_map(body, mesh=torus, in_specs=in_specs, out_specs=P(ALL), check_vma=False)
```

```python
import functools

import jax
import jax.numpy as jnp
from jax import lax
from jax.experimental import pallas as pl
from jax.experimental.pallas import tpu as pltpu
from jax.sharding import Mesh
from jax.sharding import PartitionSpec as P

TAB = 8
HOT = 8
Y, Z, C, X = "y", "z", "c", "x"
ALL = (Y, Z, C, X)
LO = 256
HEAD_ROWS = 128
BF = jnp.bfloat16
F8 = jnp.float8_e4m3fn
F32 = jnp.float32
VM = pl.BlockSpec(memory_space=pltpu.VMEM)
SM = pl.BlockSpec(memory_space=pltpu.SMEM)
LANES = (((1,), (1,)), ((), ()))


def mm(a, b):
    return jnp.dot(a, b, preferred_element_type=F32)


def mm_t(a, b):
    return lax.dot_general(a, b, LANES, preferred_element_type=F32)


def relu(a):
    return jnp.maximum(a, 0.0)


def cost(micros):
    return pl.CostEstimate(flops=int(micros * 1.0e9), bytes_accessed=1 << 20, transcendentals=0)


def params(mib):
    return pltpu.CompilerParams(vmem_limit_bytes=mib << 20)


def prepare_kernel(peers, idx_hbm, len_hbm, out_ref, idx_ref, len_ref, sem):
    copies = [
        pltpu.make_async_copy(idx_hbm, idx_ref, sem.at[0]),
        pltpu.make_async_copy(len_hbm, len_ref, sem.at[1]),
    ]
    for copy in copies:
        copy.start()
    for copy in copies:
        copy.wait()
    lens = len_ref[...]
    parts = [jnp.where(lens > h, idx_ref[:, h, :], -1) for h in range(HOT)]
    rows = jnp.concatenate(parts, axis=1)
    for t in range(TAB):
        out_ref[t * peers : (t + 1) * peers, :] = jnp.broadcast_to(
            rows[t : t + 1, :], (peers, rows.shape[1])
        )


def pack_kernel(
    w1_ref, w2_ref, w3_ref, w4_ref, dense_ref, b1_ref, b2_ref, b3_ref, table_ref, pack_ref, bottom_ref, keep_ref
):
    tail = w1_ref[HEAD_ROWS:, :]
    pack_ref[0, 0:HEAD_ROWS, :] = w1_ref[0:HEAD_ROWS, :]
    pack_ref[1, 0:HEAD_ROWS, :] = jnp.concatenate(
        [tail, jnp.zeros((HEAD_ROWS - tail.shape[0], tail.shape[1]), BF)], axis=0
    )
    for h in range(2):
        at = HEAD_ROWS
        half = w2_ref.shape[0] // 2
        pack_ref[h, at : at + half, :] = w2_ref[h * half : (h + 1) * half, :]
        at += half
        half = w3_ref.shape[0] // 2
        quarter = half // 2
        for q in range(2):
            first = h * half + q * quarter
            pack_ref[h, at : at + quarter, q * 128 : (q + 1) * 128] = w3_ref[first : first + quarter, :]
        at += quarter
        half = w4_ref.shape[1] // 2
        pack_ref[h, at : at + w4_ref.shape[0], :] = w4_ref[:, h * half : (h + 1) * half]
    lower = relu(mm(dense_ref[...], b1_ref[...])).astype(BF)
    middle = relu(mm(lower, b2_ref[...])).astype(BF)
    bottom_ref[...] = relu(mm(middle, b3_ref[...]))
    keep_ref[...] = table_ref[...]


def lookup_kernel(meta_ref, idx_ref, own_ref, other_ref, out_ref, code_ref, lo_ref, count_ref):
    peers, width = idx_ref.shape
    bags = width // HOT
    span = own_ref.shape[0]
    held = 2 * span
    his = held // LO
    rows = count_ref.shape[0]
    per_chunk = rows // bags
    z, core = meta_ref[1], meta_ref[2]
    rel = idx_ref[...] - z * held
    valid = (rel >= 0) & (rel < held)
    rel = rel ^ (core * span)
    bag = lax.broadcasted_iota(jnp.int32, (peers, width), 1) % bags
    code_ref[...] = jnp.where(valid, (rel // LO) * bags + bag, -1)
    lo_ref[...] = rel % LO
    one, zero = jnp.ones((), BF), jnp.zeros((), BF)

    def one_hot(height, ref, peer):
        ids = lax.broadcasted_iota(jnp.int16, (height, width), 0)
        return jnp.where(ids == ref[pl.ds(peer, 1), :].astype(jnp.int16), one, zero).astype(F8)

    @pl.loop(0, peers // per_chunk)
    def _(chunk):
        for g in range(per_chunk):
            peer = chunk * per_chunk + g
            left = one_hot(his * bags, code_ref, peer)
            counts = mm_t(left, one_hot(LO, lo_ref, peer)).astype(BF)
            for hi in range(his):
                count_ref[g * bags : (g + 1) * bags, hi * LO : (hi + 1) * LO] = counts[
                    hi * bags : (hi + 1) * bags
                ]
        total = mm(count_ref[:, :span], own_ref[...]) + mm(count_ref[:, span:], other_ref[...])
        out_ref[pl.ds(pl.multiple_of(chunk * rows, rows), rows), :] = total


def top_kernel(
    meta_ref, bags_ref, bottom_ref, last_ref, own_ref, side_ref, across_ref, mirror_ref,
    out_ref, in_ref, a1_ref, a2_ref, a3_ref,
):
    core, x = meta_ref[2], meta_ref[3]
    reps = last_ref.shape[0]
    peers = bags_ref.shape[0] // TAB
    bottom = bottom_ref[...]
    vectors = [bottom]
    for t in range(TAB):
        total = bags_ref[t * peers]
        for k in range(1, peers):
            total = total + bags_ref[t * peers + k]
        vectors.append(total)
    lane = lax.broadcasted_iota(jnp.int32, bottom.shape, 1)
    pairs = jnp.zeros(bottom.shape, F32)
    at = 0
    for i in range(TAB + 1):
        for j in range(i + 1, TAB + 1):
            dots = jnp.sum(vectors[i] * vectors[j], axis=1, keepdims=True)
            pairs = jnp.where(lane == at, dots, pairs)
            at += 1
    in_ref[0] = bottom.astype(BF)
    in_ref[1] = pairs.astype(BF)

    def whole(ref):
        return [(h, ref.at[h]) for h in range(2)]

    before, after = lax.rem(x + reps - 1, reps), lax.rem(x + 1, reps)
    shards = (
        (x, whole(own_ref)),
        (jnp.where(core == 0, before, after), whole(side_ref)),
        (jnp.where(core == 0, after, before), whole(mirror_ref)),
        (lax.rem(x + 2, reps), whole(across_ref)),
    )
    for owner, halves in shards:
        y = sum(mm(in_ref[h], w[0:HEAD_ROWS, :]) for h, w in halves)
        a1_ref[owner] = relu(y).astype(BF)
    base = HEAD_ROWS
    for owner, halves in shards:
        y = sum(
            mm(a1_ref[2 * h + q], w[base + q * 256 : base + (q + 1) * 256, :])
            for h, w in halves
            for q in range(2)
        )
        a2_ref[owner] = relu(y).astype(BF)
    base += 512
    for owner, halves in shards:
        y = sum(
            mm(a2_ref[2 * h + q], w[base : base + 256, q * 128 : (q + 1) * 128])
            for h, w in halves
            for q in range(2)
        )
        a3_ref[owner] = relu(y).astype(BF)
    base += 256
    logit = jnp.zeros(out_ref.shape, F32)
    for owner, halves in shards:
        y = sum(
            mm_t(a3_ref[2 * h + q], w[base : base + 64, q * 128 : (q + 1) * 128])
            for h, w in halves
            for q in range(2)
        )
        logit = logit + mm_t(last_ref[owner], relu(y).astype(BF))
    out_ref[...] = logit


def shifted(a, axis, k):
    n = lax.axis_size(axis)
    return lax.ppermute(a, axis, [(i, (i + k) % n) for i in range(n)])


def hold_kernel(in_ref, out_ref):
    pass


def held(a, micros, space):
    spec = pl.BlockSpec(memory_space=space)
    return pl.pallas_call(
        hold_kernel,
        out_shape=jax.ShapeDtypeStruct(a.shape, a.dtype),
        in_specs=[spec],
        out_specs=spec,
        input_output_aliases={0: 0},
        compiler_params=params(4),
        cost_estimate=cost(micros),
        name="held",
    )(a)


def body(tables, indices, bag_lengths, dense, b1, b2, b3, w1, w2, w3, w4, last):
    samples, width = indices.shape[0], tables.shape[1]
    reps = lax.axis_size(X)
    along_z = lax.axis_size(Z)
    peers = lax.axis_size((Y, Z))
    meta = jnp.stack([lax.axis_index(a) for a in ALL]).astype(jnp.int32)
    rows = pl.pallas_call(
        functools.partial(prepare_kernel, along_z),
        out_shape=jax.ShapeDtypeStruct((peers, HOT * samples), jnp.int32),
        in_specs=[pl.BlockSpec(memory_space=pltpu.HBM)] * 2,
        out_specs=VM,
        scratch_shapes=[
            pltpu.VMEM((TAB, HOT, samples), jnp.int32),
            pltpu.VMEM((TAB, samples), jnp.int32),
            pltpu.SemaphoreType.DMA((2,)),
        ],
        compiler_params=params(60),
        cost_estimate=cost(1),
        name="prepare",
    )(jnp.transpose(indices, (1, 2, 0)), jnp.transpose(bag_lengths))
    rows, tables, meta = lax.optimization_barrier((rows, tables, meta))
    wanted = lax.all_to_all(rows, (Y, Z), 0, 0, tiled=True)
    wanted = held(wanted, 60, pltpu.VMEM)
    w4t = jnp.transpose(w4)
    pack_rows = HEAD_ROWS + w2.shape[0] // 2 + w3.shape[0] // 4 + w4t.shape[0]
    pack, bottom, kept = pl.pallas_call(
        pack_kernel,
        out_shape=(
            jax.ShapeDtypeStruct((2, pack_rows, w2.shape[1]), BF),
            jax.ShapeDtypeStruct((samples, width), F32),
            jax.ShapeDtypeStruct(tables.shape, BF),
        ),
        in_specs=[VM] * 9,
        out_specs=(VM, VM, VM),
        compiler_params=params(8),
        cost_estimate=cost(3),
        name="pack",
    )(w1, w2, w3, w4t, dense, b1, b2, b3, tables)
    sides = [(i, (i + 1) % reps) for i in range(reps)]
    sides += [(reps + i, reps + (i - 1) % reps) for i in range(reps)]
    tables, pack = lax.optimization_barrier((tables, pack))
    other = shifted(tables, C, 1)
    side = lax.ppermute(pack, (C, X), sides)
    partial_bags = pl.pallas_call(
        lookup_kernel,
        out_shape=jax.ShapeDtypeStruct((peers * samples, width), F32),
        in_specs=[SM] + [VM] * 3,
        out_specs=VM,
        scratch_shapes=[
            pltpu.VMEM(wanted.shape, jnp.int32),
            pltpu.VMEM(wanted.shape, jnp.int32),
            pltpu.VMEM((512, 2 * tables.shape[0]), BF),
        ],
        compiler_params=params(14),
        cost_estimate=cost(40),
        name="lookup",
    )(meta, wanted, kept, other)
    side = held(side, 60, pltpu.VMEM)
    across = lax.ppermute(side, (C, X), sides)
    mirror = shifted(side, C, 1)
    bags = lax.all_to_all(
        partial_bags.reshape(peers, samples, width), (Y, Z), 0, 0, tiled=True
    )
    bags = held(bags, 15, pltpu.VMEM)
    logit = pl.pallas_call(
        top_kernel,
        out_shape=jax.ShapeDtypeStruct((1, samples), F32),
        in_specs=[SM] + [VM] * 7,
        out_specs=VM,
        scratch_shapes=[
            pltpu.VMEM((2, samples, width), BF),
            pltpu.VMEM((reps, samples, w1.shape[1]), BF),
            pltpu.VMEM((reps, samples, w2.shape[1]), BF),
            pltpu.VMEM((reps, samples, w3.shape[1]), BF),
        ],
        compiler_params=params(10),
        cost_estimate=cost(5),
        name="top",
    )(meta, bags, bottom, last.reshape(reps, 1, -1), pack, side, across, mirror)
    return logit.reshape(samples)


def solution(mesh):
    torus = Mesh(mesh.devices.reshape(8, 8, 2, mesh.shape["rep"]), ALL)
    in_specs = (
        P((Y, Z, C), None),
        P(ALL, None, None),
        P(ALL, None),
        P(ALL, None),
        P(),
        P(),
        P(),
        P(None, X),
        P(None, X),
        P(None, X),
        P(None, X),
        P(),
    )
    return jax.shard_map(body, mesh=torus, in_specs=in_specs, out_specs=P(ALL), check_vma=False)
```
